32 devices in a mesh: wave: 16 (over z, y, x), lev: 2 (over core).
Axes of the slice: x: 2, y: 2, z: 4, core: 2. Of those that a mesh axis runs over, the one named last changes fastest.
Arguments:
- fourier_in: bfloat16 [3, 28, 1280, 64], P(None, 'lev', 'wave'), may hold values from -6 to 6
- spectral_old: bfloat16 [3, 28, 16, 2816], P(None, 'lev', 'wave'), may hold values from -6 to 6
- legendre: bfloat16 [16, 1408, 1280], P('wave'), may hold values from -0.15625 to 0.15625
- g_matrix: float32 [28, 28], replicated, may hold values from -1 to 1
- modes_in: float32 [28, 28], replicated, may hold values from -1 to 1
- modes_out: float32 [28, 28], replicated, may hold values from -1 to 1
- mode_heating: float32 [28, 28], replicated, may hold values from -1 to 1
- mode_rates: float32 [28], replicated, may hold values from 0.1 to 10
- pair_ids: int32 [16], replicated, may hold values from 0 to 639, as said below
- lat_ids: int32 [1280], replicated, may hold values from 0 to 1279, each once
- limits: int32 [1280], replicated, may hold values from 10 to 1280
Outputs:
- spectral_new: bfloat16 [3, 28, 16, 2816], P(None, 'lev', 'wave')
- fourier_out: bfloat16 [3, 28, 1280, 64], P(None, 'lev', 'wave')
The draws below stay inside these ranges and needn't reach their ends.
Inputs may be any that keep to these rules, and one draw needn't show every extreme that they name: `pair_ids`: distinct pair numbers. `lat_ids`: each latitude once.
All inputs are finite; a program needn't handle non-finite values.
Results may differ from the reference program's by a relative error of at most 0.018.
Values may be sent and summed in bfloat16 or wider, within the bound.
A program may use at most 64 MiB of HBM per device.

```python
import math
import jax
import jax.numpy as jnp
from jax import lax

MMAX = 1280
NLAT = 1280
BLOCK = 64
LEV_DEV = 14
NR = 1408
NPW = 16
LEV = 28
N_LEV = 2


def draw_pair_ids(key, part):
    middle_ids = jax.random.permutation(key, MMAX // 2 - 2)[:NPW - 2].astype(jnp.int32) + 1
    end_ids = jnp.array([0, MMAX // 2 - 1], dtype=jnp.int32)
    chosen = jnp.concatenate([end_ids, middle_ids])
    shuffle = jax.random.permutation(jax.random.fold_in(key, 7), NPW)
    return chosen[shuffle]


def draw_limits(key, part):
    row_index = jnp.arange(NLAT, dtype=jnp.int32)
    from_pole = jnp.minimum(row_index, NLAT - 1 - row_index)
    jitter = jax.random.randint(key, (NLAT,), 0, 8, dtype=jnp.int32) * (from_pole > 0).astype(jnp.int32)
    return jnp.minimum(MMAX, 10 + 2 * from_pole + jitter).astype(jnp.int32)


def level_of(rng, extent, split, smallest, top_value):
    def one(axis_at, parts):
        draws = jax.random.uniform(jax.random.fold_in(jax.random.fold_in(rng, 6), axis_at), (parts,), jnp.float32, smallest / len(split), top_value / len(split))
        return jnp.repeat(jnp.exp(draws), extent[axis_at] // parts).reshape((-1,) + (1,) * (len(extent) - axis_at - 1))

    level = one(*split[0])
    for cut in split[1:]:
        level = level * one(*cut)
    return level


def centred(rng, extent, width, bound, shards=(), held_as=jnp.bfloat16):
    result = width * jax.random.normal(rng, extent, jnp.float32)
    if shards:
        result = result * level_of(rng, extent, shards, -0.22, 0.18)
    return jnp.clip(result, -bound, bound).astype(held_as)


def setup_inputs(seed: int = 0) -> dict:
    key_list = jax.random.split(jax.random.key(seed), 12)
    fourier_in = centred(key_list[0], (3, LEV, NLAT, 4 * NPW), 1.0, 6.0, ((1, 2), (2, 16)))
    spectral_old = centred(key_list[1], (3, LEV, NPW, 2 * NR), 1.0, 6.0, ((1, 2), (2, 16)))
    legendre = centred(key_list[2], (NPW, NR, NLAT), NLAT ** -0.5, 0.15625, ((0, 16),))
    g_matrix = centred(key_list[3], (LEV, LEV), LEV ** -0.5, 1.0, (), jnp.float32)
    modes_in = centred(key_list[4], (LEV, LEV), LEV ** -0.5, 1.0, (), jnp.float32)
    modes_out = centred(key_list[5], (LEV, LEV), LEV ** -0.5, 1.0, (), jnp.float32)
    mode_heating = centred(key_list[6], (LEV, LEV), LEV ** -0.5, 1.0, (), jnp.float32)
    mode_rates = jnp.clip(jnp.exp(jax.random.uniform(key_list[7], (LEV,), jnp.float32, math.log(0.1), math.log(10.0))), 0.1, 10.0)
    pair_ids = draw_pair_ids(jax.random.fold_in(key_list[11], 71), 0)
    lat_ids = jax.random.permutation(key_list[9], NLAT).astype(jnp.int32)
    limits = draw_limits(jax.random.fold_in(key_list[11], 71), 0)
    return dict(fourier_in=fourier_in, spectral_old=spectral_old, legendre=legendre, g_matrix=g_matrix, modes_in=modes_in, modes_out=modes_out, mode_heating=mode_heating, mode_rates=mode_rates, pair_ids=pair_ids, lat_ids=lat_ids, limits=limits)


coupling = 2.0
highest = lax.Precision.HIGHEST


def pair_layout(pair_number, row_count):
    row_index = jnp.arange(row_count, dtype=jnp.int32)
    first_length = MMAX - pair_number
    first_pad = ((first_length + BLOCK - 1) // BLOCK) * BLOCK
    in_first = row_index < first_pad
    row_valid = jnp.where(in_first, row_index < first_length, row_index - first_pad < pair_number + 1)
    degree = jnp.where(in_first, pair_number + row_index, MMAX - 1 - pair_number + row_index - first_pad).astype(jnp.float32)
    lfactor = degree * (degree + 1.0) / float(MMAX * (MMAX - 1))
    return row_valid, lfactor, first_pad


def grouped_levels(matrix, vector, group_count, lev_count):
    matrix_groups = matrix.reshape(matrix.shape[0], group_count, lev_count)
    vector_groups = vector.reshape(group_count, lev_count, vector.shape[1])
    partials = jnp.einsum("ogl,glx->gox", matrix_groups, vector_groups, precision=highest, preferred_element_type=jnp.float32)
    partials = lax.optimization_barrier(partials.astype(jnp.bfloat16))
    return jnp.sum(partials.astype(jnp.float32), axis=0)


def reference(fourier_in, spectral_old, legendre, g_matrix, modes_in, modes_out, mode_heating, mode_rates, pair_ids, lat_ids, limits):
    row_count = MMAX + 2 * BLOCK
    row_valid, lfactor, first_pad = jax.vmap(lambda pair_number: pair_layout(pair_number, row_count))(pair_ids)
    in_first = jnp.arange(row_count, dtype=jnp.int32)[None, :] < first_pad[:, None]
    row_limit = limits[lat_ids]
    both_waves = jnp.stack([pair_ids, MMAX - 1 - pair_ids], axis=1)
    column_wave = jnp.repeat(both_waves, 2, axis=1).reshape(-1)
    keep_mask = column_wave[None, :] < row_limit[:, None]
    masked = jnp.where(keep_mask[None, None], fourier_in, jnp.zeros((), fourier_in.dtype))
    slot_major = jnp.moveaxis(masked.reshape(3, LEV, NLAT, NPW, 2, 2), 3, 0)

    def forward_slot(operands):
        slot_data, pair_table, slot_first, slot_valid = operands
        table_wide = pair_table.astype(jnp.float32)
        data_wide = slot_data.astype(jnp.float32)
        first_wave = jnp.einsum("fljc,rj->flcr", data_wide[:, :, :, 0], table_wide, precision=highest)
        second_wave = jnp.einsum("fljc,rj->flcr", data_wide[:, :, :, 1], table_wide, precision=highest)
        chosen = jnp.where(slot_first[None, None, None, :], first_wave, second_wave)
        return jnp.where(slot_valid[None, None, None, :], chosen, 0.0)

    tendency = lax.map(forward_slot, (slot_major, legendre, in_first, row_valid))
    tendency = jnp.moveaxis(tendency, 0, 2)
    flat_size = NPW * 2 * row_count
    old_fields = spectral_old.reshape(3, LEV, NPW, 2, row_count).astype(jnp.float32)
    vorticity = (old_fields[0] + tendency[0]).reshape(LEV, flat_size)
    divergence = (old_fields[1] + tendency[1]).reshape(LEV, flat_size)
    heat_star = (old_fields[2] + tendency[2]).reshape(LEV, flat_size)
    wave_factor = jnp.broadcast_to(lfactor[:, None, :], (NPW, 2, row_count)).reshape(1, flat_size)
    keep_rows = jnp.broadcast_to(row_valid[:, None, :], (NPW, 2, row_count)).reshape(1, flat_size)
    hydrostatic = grouped_levels(g_matrix, heat_star, N_LEV, LEV_DEV)
    right_side = divergence + coupling * wave_factor * hydrostatic
    projected = grouped_levels(modes_in, right_side, N_LEV, LEV_DEV)
    modal_part = projected / (1.0 + coupling * coupling * wave_factor * mode_rates[:, None])
    divergence_new = grouped_levels(modes_out, modal_part, N_LEV, LEV_DEV)
    heat_change = grouped_levels(mode_heating, modal_part, N_LEV, LEV_DEV)
    vorticity_out = jnp.where(keep_rows, vorticity, 0.0).astype(jnp.bfloat16)
    divergence_out = jnp.where(keep_rows, divergence_new, 0.0).astype(jnp.bfloat16)
    heat_out = jnp.where(keep_rows, heat_star - coupling * heat_change, 0.0).astype(jnp.bfloat16)
    spectral_new = jnp.stack([vorticity_out, divergence_out, heat_out]).reshape(3, LEV, NPW, 2 * row_count)
    new_slots = jnp.moveaxis(spectral_new.reshape(3, LEV, NPW, 2, row_count), 2, 0)

    def inverse_slot(operands):
        slot_spectra, pair_table, slot_first = operands
        spectra_wide = slot_spectra.astype(jnp.float32)
        table_wide = pair_table.astype(jnp.float32)
        first_rows = jnp.where(slot_first[None, None, None, :], spectra_wide, 0.0)
        second_rows = jnp.where(jnp.logical_not(slot_first)[None, None, None, :], spectra_wide, 0.0)
        first_wave = jnp.einsum("flcr,rj->fljc", first_rows, table_wide, precision=highest)
        second_wave = jnp.einsum("flcr,rj->fljc", second_rows, table_wide, precision=highest)
        return jnp.stack([first_wave, second_wave], axis=3).reshape(3, LEV, NLAT, 4)

    gridded = lax.map(inverse_slot, (new_slots, legendre, in_first))
    gridded = jnp.moveaxis(gridded, 0, 3).reshape(3, LEV, NLAT, 4 * NPW)
    fourier_out = jnp.where(keep_mask[None, None], gridded, 0.0).astype(jnp.bfloat16)
    return (spectral_new, fourier_out)
```

```python
import functools

import jax
import jax.numpy as jnp
from jax import lax
from jax.experimental import pallas as pl
from jax.experimental.pallas import tpu as pltpu
from jax.sharding import PartitionSpec as P

MMAX = 1280
BLOCK = 64
K = 8
CHUNK = 16
F32, BF16 = jnp.float32, jnp.bfloat16
MESH = pl.DeviceIdType.MESH
HI = lax.Precision.HIGHEST
NT = (((1,), (1,)), ((), ()))


def iota(shape, dim):
    return lax.broadcasted_iota(jnp.int32, shape, dim)


def dot(a, b):
    return jnp.dot(a, b, preferred_element_type=F32)


def fdot(a, b):
    return jnp.dot(a, b, precision=HI, preferred_element_type=F32)


def onehot(mask, dtype=BF16):
    return jnp.where(mask, 1.0, 0.0).astype(dtype)


def split3(left, right):
    lh = left.astype(BF16)
    ll = (left - lh.astype(F32)).astype(BF16)
    rh = right.astype(BF16)
    rl = (right - rh.astype(F32)).astype(BF16)
    return jnp.concatenate([lh, lh, ll], axis=1), jnp.concatenate([rh, rl, rh], axis=0)


def make_slots(lev_n):
    fill = -2 * lev_n % K
    slots = []
    for c in range(2):
        slots += [(f, l, c) for f in (1, 2) for l in range(lev_n)] + [(0, l, c) for l in range(fill)]
    rest = list(range(fill, lev_n))
    whole = len(rest) // K * K
    for c in range(2):
        slots += [(0, l, c) for l in rest[:whole]]
    for c in range(2):
        slots += [(0, l, c) for l in rest[whole:]]
    return [slots[i : i + K] for i in range(0, len(slots), K)]


def make_pieces(lev_n, jl):
    groups = make_slots(lev_n)
    td = (2 * lev_n + K - 1) // K
    ends = [td, 2 * td, len(groups)]
    lanes = (len(groups) * jl + 127) // 128 * 128
    up = [min((e * jl + 127) // 128 * 128, lanes) for e in ends]
    down = [e * jl // 128 * 128 for e in ends[:2]] + [lanes]
    return groups, [0] + ends, lanes, [0] + up, [0] + down


def kernel(
    n, nlev, x_hbm, old_hbm, leg_hbm, g_hbm, mi_hbm, mo_hbm, mh_hbm, rates_hbm, pid_hbm, lat_hbm, lim_hbm,
    spec_hbm, recv2,
    spec_ref, x_ref, old_ref, leg, g_ref, mi_ref, mo_ref, mh_ref, rates_ref, pid_ref, lat_ref, lim_ref,
    send1, recv1, send2, es, er, hot,
    out_sem, in_sem, s1, r1, s2, r2, es_sem, er_sem,
):
    lev_n = x_ref.shape[1]
    jl = x_ref.shape[3]
    groups, ends, lanes, up, down = make_pieces(lev_n, jl)
    nr, nlat = leg_hbm.shape[1:]
    me, lev = lax.axis_index("wave"), lax.axis_index("lev")
    other = lax.rem(lev + 1, nlev)
    plane = n // 4
    z, xy = me // plane, lax.rem(me, plane)
    low = z < 2

    def target(i):
        zi, k = i // plane, lax.rem(i, plane)
        far = jnp.where(low, 3 - zi, zi)
        near = jnp.where(zi == 2, z + 1 - 2 * lax.rem(z, 2), z)
        tz = jnp.where(zi < 2, far, near)
        return tz * plane + lax.rem(xy + k + zi // 3, plane)

    barrier = pltpu.get_barrier_semaphore()

    def greet(i, carry):
        pl.semaphore_signal(barrier, inc=1, device_id=(target(i), lev), device_id_type=MESH)
        return carry

    lax.fori_loop(0, n - 1, greet, 0)
    pl.semaphore_signal(barrier, inc=1, device_id=(me, other), device_id_type=MESH)

    pairs = [(x_hbm.at[f], x_ref.at[f]) for f in (1, 2, 0)] + [
        (pid_hbm, pid_ref), (lat_hbm, lat_ref), (lim_hbm, lim_ref), (g_hbm, g_ref), (mi_hbm, mi_ref),
        (mo_hbm, mo_ref), (mh_hbm, mh_ref), (rates_hbm, rates_ref), (old_hbm, old_ref), (leg_hbm.at[0], leg),
    ]
    loads = [pltpu.make_async_copy(src, dst, in_sem.at[i]) for i, (src, dst) in enumerate(pairs)]
    for load in loads:
        load.start()
    for load in loads[:3]:
        load.wait()

    pr, pc = iota((CHUNK * 16, 4 * CHUNK * K), 0), iota((CHUNK * 16, 4 * CHUNK * K), 1)
    base = pr % K * (4 * CHUNK) + pr // 16 * 4 + pr // 8 % 2 * 2

    def packed(g, h):
        slots = groups[g]
        part = jnp.zeros(pr.shape, jnp.int32)
        for k, (f, l, c) in enumerate(slots):
            if c:
                part = jnp.where(pr % K == k, 1, part)
        perm = onehot(pc == base + part)
        blocks = [x_ref[f, l, h * 4 * CHUNK : (h + 1) * 4 * CHUNK] for f, l, c in slots]
        blocks += [jnp.zeros_like(blocks[0])] * (K - len(slots))
        return perm, jnp.concatenate(blocks, axis=0)

    def pack_run(first, last, h):
        out, g = [], first
        while g < last:
            run = [g]
            parts = {c for f, l, c in groups[g]}
            while len(parts) == 1 and run[-1] + 1 < last and {c for f, l, c in groups[run[-1] + 1]} == parts and len(groups[run[-1] + 1]) == len(groups[g]):
                run.append(run[-1] + 1)
            perm = packed(g, h)[0]
            data = jnp.concatenate([packed(i, h)[1] for i in run], axis=1) if len(run) > 1 else packed(g, h)[1]
            out.append(dot(perm, data).astype(BF16))
            g = run[-1] + 1
        return out

    def copy1(p, to):
        at = pl.ds(up[p], up[p + 1] - up[p])
        return pltpu.make_async_remote_copy(
            src_ref=send1.at[to, :, at], dst_ref=recv1.at[me, :, at], send_sem=s1.at[p], recv_sem=r1.at[p],
            device_id=(to, lev), device_id_type=MESH,
        )

    def copy2(p, to):
        at = pl.ds(down[p], down[p + 1] - down[p])
        return pltpu.make_async_remote_copy(
            src_ref=send2.at[to, :, at], dst_ref=recv2.at[me, :, at], send_sem=s2.at[p], recv_sem=r2.at[p],
            device_id=(to, lev), device_id_type=MESH,
        )

    def start_all(copy, p):
        def start(i, carry):
            copy(p, target(i)).start()
            return carry

        lax.fori_loop(0, n - 1, start, 0)

    def whole(src, dst, bounds, ss, rr, p):
        at = pl.ds(bounds[p], bounds[p + 1] - bounds[p])
        return pltpu.make_async_remote_copy(
            src_ref=src.at[pl.ds(0, n - 1), :, at], dst_ref=dst.at[pl.ds(0, n - 1), :, at], send_sem=ss.at[p],
            recv_sem=rr.at[p], device_id=(me, other), device_id_type=MESH,
        )

    kept = [None] * (n // CHUNK)
    done = 0
    for p in range(3):
        lo, hi = up[p], up[p + 1]
        if hi > lo:
            last = min(len(groups), (hi + jl - 1) // jl)
            for h in range(n // CHUNK):
                rows = [] if kept[h] is None else [kept[h]]
                rows += pack_run(done, last, h)
                row = jnp.concatenate(rows, axis=1) if len(rows) > 1 else rows[0]
                if row.shape[1] < hi - lo:
                    row = jnp.concatenate([row, jnp.zeros((row.shape[0], hi - lo - row.shape[1]), BF16)], axis=1)
                send1[h * CHUNK : (h + 1) * CHUNK, :, lo:hi] = row[:, : hi - lo].reshape(CHUNK, 16, hi - lo)
                kept[h] = row[:, hi - lo :] if row.shape[1] > hi - lo else None
            done = last
            if p == 0:
                pl.semaphore_wait(barrier, n)
            start_all(copy1, p)
            recv1[me, :, lo:hi] = send1[me, :, lo:hi]

    for load in loads[3:12]:
        load.wait()

    hr = iota((16, nlat), 0)
    lim = lim_ref[...][None, :]
    lim_rows = jnp.where(hr == 0, lim // 8, jnp.where(hr == 1, lim % 8, 0)).astype(F32).astype(BF16)
    hot[...] = onehot(iota((nlat, nlat), 0) == lat_ref[...][None, :])
    got = dot(lim_rows, hot[...])
    row_limit = got[0:1] * 8.0 + got[1:2]
    a = pid_ref[me]
    wave = jnp.where(hr < 8, a, MMAX - 1 - a).astype(F32)
    keep = onehot(wave < row_limit, F32)
    keep_b = keep.astype(BF16)

    r = iota((1, nr), 1)
    first_pad = (MMAX - a + BLOCK - 1) // BLOCK * BLOCK
    first = r < first_pad
    used = (first & (r < MMAX - a)) | ((r >= first_pad) & (r - first_pad <= a))
    degree = jnp.where(first, a + r, MMAX - 1 - a + r - first_pad).astype(F32)
    lam = degree * (degree + 1.0) / float(MMAX * (MMAX - 1))

    levels = nlev * lev_n
    half = (levels + 15) // 16 * 16
    td = ends[1] * K
    mode = onehot(iota((half, levels), 0) == iota((half, levels), 1), F32)
    mode_t = onehot(iota((levels, half), 0) == iota((levels, half), 1), F32)
    own = lev_n * lev
    li, si = iota((levels, td), 0), iota((levels, td), 1)
    pick_div = onehot((li == own + si) & (si < lev_n), F32)
    pick_heat = onehot((li == own + si - lev_n) & (si >= lev_n) & (si < 2 * lev_n), F32)
    si, li = iota((td, levels), 0), iota((td, levels), 1)
    pick_div_t = onehot((li == own + si) & (si < lev_n), F32)
    pick_heat_t = onehot((li == own + si - lev_n) & (si >= lev_n) & (si < 2 * lev_n), F32)
    m_in = mi_ref[...]
    w1 = jnp.concatenate(
        [fdot(fdot(mode, m_in), pick_div), fdot(fdot(mode, fdot(m_in, g_ref[...])), pick_heat)], axis=0
    )
    w2 = fdot(fdot(pick_div_t, mo_ref[...]), mode_t) - 2.0 * fdot(fdot(pick_heat_t, mh_ref[...]), mode_t)
    rates = jnp.sum(
        jnp.where(iota((half, levels), 0) == iota((half, levels), 1), rates_ref[...][None, :], 0.0),
        axis=1, keepdims=True,
    )
    si = iota((td, 1), 0)
    stays = onehot(si >= lev_n, F32)

    def old_rows(p):
        slots = [s for g in groups[ends[p] : ends[p + 1]] for s in g]
        rows = (ends[p + 1] - ends[p]) * K
        total = None
        for c in range(2):
            if not any(s[2] == c for s in slots):
                continue
            row, col = iota((rows, 3 * lev_n), 0), iota((rows, 3 * lev_n), 1)
            src = jnp.full(row.shape, -1, jnp.int32)
            start = 0
            while start < len(slots):
                f, l, cc = slots[start]
                stop = start
                while stop < len(slots) and slots[stop] == (f, l + stop - start, cc):
                    stop += 1
                if cc == c:
                    src = jnp.where((row >= start) & (row < stop), row - start + f * lev_n + l, src)
                start = stop
            part = dot(onehot(col == src), old_all[:, c * nr : (c + 1) * nr])
            total = part if total is None else total + part
        return total

    old_all = jnp.concatenate([old_ref[f, 0] for f in range(3)], axis=0)
    olds = [old_rows(p) for p in range(3)]
    loads[12].wait()

    def forward(p):
        g_n = ends[p + 1] - ends[p]
        cols = jnp.concatenate(
            [
                jnp.concatenate([recv1[d, :, g * jl : (g + 1) * jl] for d in range(n)], axis=1) * keep_b
                for g in range(ends[p], ends[p + 1])
            ],
            axis=0,
        )
        both = lax.dot_general(cols, leg[...], NT, preferred_element_type=F32).reshape(g_n, 2, K, nr)
        total = jnp.where(iota((g_n, K, nr), 2) < first_pad, both[:, 0], both[:, 1]).reshape(g_n * K, nr)
        return jnp.where(used, olds[p] + total, 0.0)

    def inverse(p, new):
        g_n = ends[p + 1] - ends[p]
        sides = jnp.stack(
            [
                jnp.where(first, new, 0.0).reshape(g_n, K, nr),
                jnp.where(first, 0.0, new).reshape(g_n, K, nr),
            ],
            axis=1,
        ).reshape(g_n * 16, nr).astype(BF16)
        out = dot(sides, leg[...])
        return [(out[i * 16 : (i + 1) * 16] * keep).astype(BF16) for i in range(g_n)]

    def exchange(p):
        return pltpu.make_async_remote_copy(
            src_ref=es.at[p], dst_ref=er.at[p], send_sem=es_sem.at[p], recv_sem=er_sem.at[p],
            device_id=(me, other), device_id_type=MESH,
        )

    grids = []

    def send_piece(p):
        lo, hi = down[p], down[p + 1]
        if hi == lo:
            return
        for d in range(n):
            parts, at = [], lo
            while at < hi:
                g = at // jl
                if g >= len(grids):
                    parts.append(jnp.zeros((16, hi - at), BF16))
                    break
                stop = min(hi, (g + 1) * jl)
                parts.append(grids[g][:, d * jl + at - g * jl : d * jl + stop - g * jl])
                at = stop
            send2[d, :, lo:hi] = jnp.concatenate(parts, axis=1) if len(parts) > 1 else parts[0]
        start_all(copy2, p)

    news = []
    for p in range(3):
        if up[p + 1] > up[p]:
            whole(send1, recv1, up, s1, r1, p).wait_recv()
        total = forward(p)
        if p < 2:
            w1s, ts = split3(w1, total)
            res = dot(w1s, ts)
            proj = res[:half] + 2.0 * lam * res[half:]
            es[p] = proj.astype(BF16)
            exchange(p).start()
            exchange(p).wait()
            modal = (proj + er[p].astype(F32)) / (1.0 + 4.0 * lam * rates)
            w2s, ms = split3(w2, modal)
            total = jnp.where(used, total * stays + dot(w2s, ms), 0.0)
        grids += inverse(p, total)
        news.append(total)
        send_piece(p)

    own_copy = pltpu.make_async_copy(send2.at[me], recv2.at[me], out_sem.at[0])
    own_copy.start()

    flat = [s for g in groups for s in g]
    starts = [e * K for e in ends]

    def row_of(slot):
        i = flat.index(slot)
        p = max(j for j in range(3) if starts[j] <= i)
        return p, i - starts[p]

    for c in range(2):
        for f in range(3):
            parts, l = [], 0
            while l < lev_n:
                p, i = row_of((f, l, c))
                stop = l
                while stop < lev_n and row_of((f, stop, c)) == (p, i + stop - l):
                    stop += 1
                parts.append(news[p][i : i + stop - l])
                l = stop
            rows = jnp.concatenate(parts, axis=0) if len(parts) > 1 else parts[0]
            spec_ref[f, 0, :, c * nr : (c + 1) * nr] = rows.astype(BF16)
    spec_copy = pltpu.make_async_copy(spec_ref, spec_hbm, out_sem.at[1])
    spec_copy.start()

    for p in range(3):
        if up[p + 1] > up[p]:
            whole(send1, recv1, up, s1, r1, p).wait_send()
        if down[p + 1] > down[p]:
            whole(send2, recv2, down, s2, r2, p).wait_send()
    own_copy.wait()
    spec_copy.wait()
    for p in range(3):
        if down[p + 1] > down[p]:
            whole(send2, recv2, down, s2, r2, p).wait_recv()


def finish(n, lev_n, jl, got_hbm, spec_in, spec_hbm, out_hbm, got, out_ref, got_sem, sem):
    groups, ends, lanes, up, down = make_pieces(lev_n, jl)
    spec_copy = pltpu.make_async_copy(spec_in, spec_hbm, sem.at[3])
    load = pltpu.make_async_copy(got_hbm, got, got_sem)
    load.start()
    spec_copy.start()
    load.wait()
    where = {s: (g, k) for g, slots in enumerate(groups) for k, s in enumerate(slots)}
    pr, pc = iota((4 * CHUNK * K, 2 * CHUNK * 16), 0), iota((4 * CHUNK * K, 2 * CHUNK * 16), 1)
    q = pr % (4 * CHUNK)
    perm = onehot(pc == q % 2 * (CHUNK * 16) + q // 4 * 16 + q // 2 % 2 * 8 + pr // (4 * CHUNK))
    paired, single = [], {}
    for g, slots in enumerate(groups):
        partners = {where[(f, l, 1)] for f, l, c in slots if c == 0}
        if all(c == 0 for f, l, c in slots) and len({b for b, k in partners}) == 1:
            b = next(iter(partners))[0]
            if all(where[(f, l, 1)] == (b, k) for k, (f, l, c) in enumerate(slots)):
                paired.append((g, b))
    covered = {g for pair in paired for g in pair}
    for g, slots in enumerate(groups):
        if g not in covered:
            single[g] = slots
    for h in range(n // CHUNK):
        rows = got[h * CHUNK : (h + 1) * CHUNK].reshape(CHUNK * 16, lanes)
        qs = slice(h * 4 * CHUNK, (h + 1) * 4 * CHUNK)
        tops = jnp.concatenate([rows[:, g * jl : (g + 1) * jl] for g, b in paired], axis=1)
        bots = jnp.concatenate([rows[:, b * jl : (b + 1) * jl] for g, b in paired], axis=1)
        back = dot(perm, jnp.concatenate([tops, bots], axis=0)).astype(BF16)
        for i, (g, b) in enumerate(paired):
            for k, (f, l, c) in enumerate(groups[g]):
                out_ref[f, l, qs] = back[k * 4 * CHUNK : (k + 1) * 4 * CHUNK, i * jl : (i + 1) * jl]
        for g, slots in single.items():
            zero = [(f, l) for f, l, c in slots if c == 0]
            count = len(zero)
            sr, sc = iota((4 * CHUNK * count, CHUNK * 16), 0), iota((4 * CHUNK * count, CHUNK * 16), 1)
            sq, sk = sr % (4 * CHUNK), sr // (4 * CHUNK)
            some = onehot(sc == sq // 4 * 16 + sq // 2 % 2 * 8 + sk + count * (sq % 2))
            back = dot(some, rows[:, g * jl : (g + 1) * jl]).astype(BF16)
            for k, (f, l) in enumerate(zero):
                out_ref[f, l, qs] = back[k * 4 * CHUNK : (k + 1) * 4 * CHUNK]
    copies = [pltpu.make_async_copy(out_ref.at[f], out_hbm.at[f], sem.at[f]) for f in range(3)]
    for copy in copies:
        copy.start()
    for copy in copies:
        copy.wait()
    spec_copy.wait()


def body(
    fourier_in, spectral_old, legendre, g_matrix, modes_in, modes_out, mode_heating, mode_rates, pair_ids, lat_ids,
    limits,
):
    n, nlev = lax.axis_size("wave"), lax.axis_size("lev")
    fields, lev_n, jl, q_n = fourier_in.shape
    groups, ends, lanes, up, down = make_pieces(lev_n, jl)
    nr, nlat = legendre.shape[1:]
    half = (nlev * lev_n + 15) // 16 * 16
    hbm = pl.BlockSpec(memory_space=pltpu.HBM)
    spec, got = pl.pallas_call(
        functools.partial(kernel, n, nlev),
        out_shape=(
            jax.ShapeDtypeStruct((fields, 1, lev_n, 2 * nr), BF16),
            jax.ShapeDtypeStruct((n, 16, lanes), BF16),
        ),
        in_specs=[hbm] * 11,
        out_specs=(hbm, hbm),
        scratch_shapes=[
            pltpu.VMEM((fields, 1, lev_n, 2 * nr), BF16),
            pltpu.VMEM((fields, lev_n, q_n, jl), BF16),
            pltpu.VMEM((fields, 1, lev_n, 2 * nr), BF16),
            pltpu.VMEM((nr, nlat), BF16),
            pltpu.VMEM(g_matrix.shape, F32),
            pltpu.VMEM(g_matrix.shape, F32),
            pltpu.VMEM(g_matrix.shape, F32),
            pltpu.VMEM(g_matrix.shape, F32),
            pltpu.VMEM(mode_rates.shape, F32),
            pltpu.SMEM(pair_ids.shape, jnp.int32),
            pltpu.VMEM(lat_ids.shape, jnp.int32),
            pltpu.VMEM(limits.shape, jnp.int32),
            pltpu.VMEM((n, 16, lanes), BF16),
            pltpu.VMEM((n, 16, lanes), BF16),
            pltpu.VMEM((n, 16, lanes), BF16),
            pltpu.VMEM((2, half, nr), BF16),
            pltpu.VMEM((2, half, nr), BF16),
            pltpu.VMEM((nlat, nlat), BF16),
            pltpu.SemaphoreType.DMA((2,)),
            pltpu.SemaphoreType.DMA((13,)),
            pltpu.SemaphoreType.DMA((3,)),
            pltpu.SemaphoreType.DMA((3,)),
            pltpu.SemaphoreType.DMA((3,)),
            pltpu.SemaphoreType.DMA((3,)),
            pltpu.SemaphoreType.DMA((2,)),
            pltpu.SemaphoreType.DMA((2,)),
        ],
        compiler_params=pltpu.CompilerParams(
            collective_id=0, has_side_effects=True, vmem_limit_bytes=48 * 1024 * 1024
        ),
        cost_estimate=pl.CostEstimate(flops=10**9, bytes_accessed=8 * 10**6, transcendentals=0),
    )(
        jnp.transpose(fourier_in, (0, 1, 3, 2)),
        jnp.transpose(spectral_old, (0, 2, 1, 3)),
        legendre,
        g_matrix,
        modes_in,
        modes_out,
        mode_heating,
        mode_rates,
        pair_ids,
        lat_ids,
        limits,
    )
    spec, out = pl.pallas_call(
        functools.partial(finish, n, lev_n, jl),
        out_shape=(
            jax.ShapeDtypeStruct((fields, 1, lev_n, 2 * nr), BF16),
            jax.ShapeDtypeStruct((fields, lev_n, q_n, jl), BF16),
        ),
        in_specs=[hbm] * 2,
        out_specs=(hbm, hbm),
        scratch_shapes=[
            pltpu.VMEM((n, 16, lanes), BF16),
            pltpu.VMEM((fields, lev_n, q_n, jl), BF16),
            pltpu.SemaphoreType.DMA,
            pltpu.SemaphoreType.DMA((4,)),
        ],
        compiler_params=pltpu.CompilerParams(vmem_limit_bytes=48 * 1024 * 1024),
        cost_estimate=pl.CostEstimate(flops=2 * 10**8, bytes_accessed=2 * 10**6, transcendentals=0),
    )(got, spec)
    return jnp.transpose(spec, (0, 2, 1, 3)), jnp.transpose(out, (0, 1, 3, 2))


def solution(mesh):
    wave = P(None, "lev", "wave", None)
    return jax.shard_map(
        body,
        mesh=mesh,
        in_specs=(wave, wave, P("wave", None, None)) + (P(),) * 8,
        out_specs=(wave, wave),
        check_vma=False,
    )
```

```python
import functools

import jax
import jax.numpy as jnp
from jax import lax
from jax.experimental import pallas as pl
from jax.experimental.pallas import tpu as pltpu
from jax.sharding import PartitionSpec as P

MMAX = 1280
BLOCK = 64
K = 8
CHUNK = 16
F32, BF16 = jnp.float32, jnp.bfloat16
MESH = pl.DeviceIdType.MESH
HI = lax.Precision.HIGHEST
NT = (((1,), (1,)), ((), ()))


def iota(shape, dim):
    return lax.broadcasted_iota(jnp.int32, shape, dim)


def dot(a, b):
    return jnp.dot(a, b, preferred_element_type=F32)


def fdot(a, b):
    return jnp.dot(a, b, precision=HI, preferred_element_type=F32)


def onehot(mask, dtype=BF16):
    return jnp.where(mask, 1.0, 0.0).astype(dtype)


def split3(left, right):
    lh = left.astype(BF16)
    ll = (left - lh.astype(F32)).astype(BF16)
    rh = right.astype(BF16)
    rl = (right - rh.astype(F32)).astype(BF16)
    return jnp.concatenate([lh, lh, ll], axis=1), jnp.concatenate([rh, rl, rh], axis=0)


def make_slots(lev_n):
    fill = -2 * lev_n % K
    slots = []
    for c in range(2):
        slots += [(f, l, c) for f in (1, 2) for l in range(lev_n)] + [(0, l, c) for l in range(fill)]
    rest = list(range(fill, lev_n))
    whole = len(rest) // K * K
    for c in range(2):
        slots += [(0, l, c) for l in rest[:whole]]
    for c in range(2):
        slots += [(0, l, c) for l in rest[whole:]]
    return [slots[i : i + K] for i in range(0, len(slots), K)]


def make_pieces(lev_n, jl):
    groups = make_slots(lev_n)
    td = (2 * lev_n + K - 1) // K
    ends = [td, 2 * td, len(groups)]
    lanes = (len(groups) * jl + 127) // 128 * 128
    up = [min((e * jl + 127) // 128 * 128, lanes) for e in ends]
    down = [e * jl // 128 * 128 for e in ends[:2]] + [lanes]
    return groups, [0] + ends, lanes, [0] + up, [0] + down


def kernel(
    n, nlev, x_hbm, old_hbm, leg_hbm, g_hbm, mi_hbm, mo_hbm, mh_hbm, rates_hbm, pid_hbm, lat_hbm, lim_hbm,
    spec_hbm, recv2,
    spec_ref, x_ref, old_ref, leg, g_ref, mi_ref, mo_ref, mh_ref, rates_ref, pid_ref, lat_ref, lim_ref,
    send1, recv1, send2, es, er, hot,
    out_sem, in_sem, s1, r1, s2, r2, es_sem, er_sem,
):
    lev_n = x_ref.shape[1]
    jl = x_ref.shape[3]
    groups, ends, lanes, up, down = make_pieces(lev_n, jl)
    nr, nlat = leg_hbm.shape[1:]
    me, lev = lax.axis_index("wave"), lax.axis_index("lev")
    other = lax.rem(lev + 1, nlev)
    plane = n // 4
    z, xy = me // plane, lax.rem(me, plane)
    low = z < 2

    def target(i):
        zi, k = i // plane, lax.rem(i, plane)
        far = jnp.where(low, 3 - zi, zi)
        near = jnp.where(zi == 2, z + 1 - 2 * lax.rem(z, 2), z)
        tz = jnp.where(zi < 2, far, near)
        return tz * plane + lax.rem(xy + k + zi // 3, plane)

    barrier = pltpu.get_barrier_semaphore()

    def greet(i, carry):
        pl.semaphore_signal(barrier, inc=1, device_id=(target(i), lev), device_id_type=MESH)
        return carry

    lax.fori_loop(0, n - 1, greet, 0)
    pl.semaphore_signal(barrier, inc=1, device_id=(me, other), device_id_type=MESH)

    pairs = [(x_hbm.at[f], x_ref.at[f]) for f in (1, 2, 0)] + [
        (pid_hbm, pid_ref), (lat_hbm, lat_ref), (lim_hbm, lim_ref), (g_hbm, g_ref), (mi_hbm, mi_ref),
        (mo_hbm, mo_ref), (mh_hbm, mh_ref), (rates_hbm, rates_ref), (old_hbm, old_ref), (leg_hbm.at[0], leg),
    ]
    loads = [pltpu.make_async_copy(src, dst, in_sem.at[i]) for i, (src, dst) in enumerate(pairs)]
    for load in loads:
        load.start()
    for load in loads[:3]:
        load.wait()

    pr, pc = iota((CHUNK * 16, 4 * CHUNK * K), 0), iota((CHUNK * 16, 4 * CHUNK * K), 1)
    base = pr % K * (4 * CHUNK) + pr // 16 * 4 + pr // 8 % 2 * 2

    def packed(g, h):
        slots = groups[g]
        part = jnp.zeros(pr.shape, jnp.int32)
        for k, (f, l, c) in enumerate(slots):
            if c:
                part = jnp.where(pr % K == k, 1, part)
        perm = onehot(pc == base + part)
        blocks = [x_ref[f, l, h * 4 * CHUNK : (h + 1) * 4 * CHUNK] for f, l, c in slots]
        blocks += [jnp.zeros_like(blocks[0])] * (K - len(slots))
        return perm, jnp.concatenate(blocks, axis=0)

    def pack_run(first, last, h):
        out, g = [], first
        while g < last:
            run = [g]
            parts = {c for f, l, c in groups[g]}
            while len(parts) == 1 and run[-1] + 1 < last and {c for f, l, c in groups[run[-1] + 1]} == parts and len(groups[run[-1] + 1]) == len(groups[g]):
                run.append(run[-1] + 1)
            perm = packed(g, h)[0]
            data = jnp.concatenate([packed(i, h)[1] for i in run], axis=1) if len(run) > 1 else packed(g, h)[1]
            out.append(dot(perm, data).astype(BF16))
            g = run[-1] + 1
        return out

    def copy1(p, to):
        at = pl.ds(up[p], up[p + 1] - up[p])
        return pltpu.make_async_remote_copy(
            src_ref=send1.at[to, :, at], dst_ref=recv1.at[me, :, at], send_sem=s1.at[p], recv_sem=r1.at[p],
            device_id=(to, lev), device_id_type=MESH,
        )

    def copy2(p, to):
        at = pl.ds(down[p], down[p + 1] - down[p])
        return pltpu.make_async_remote_copy(
            src_ref=send2.at[to, :, at], dst_ref=recv2.at[me, :, at], send_sem=s2.at[p], recv_sem=r2.at[p],
            device_id=(to, lev), device_id_type=MESH,
        )

    def start_all(copy, p):
        def start(i, carry):
            copy(p, target(i)).start()
            return carry

        lax.fori_loop(0, n - 1, start, 0)

    def whole(src, dst, bounds, ss, rr, p):
        at = pl.ds(bounds[p], bounds[p + 1] - bounds[p])
        return pltpu.make_async_remote_copy(
            src_ref=src.at[pl.ds(0, n - 1), :, at], dst_ref=dst.at[pl.ds(0, n - 1), :, at], send_sem=ss.at[p],
            recv_sem=rr.at[p], device_id=(me, other), device_id_type=MESH,
        )

    kept = [None] * (n // CHUNK)
    done = 0
    for p in range(3):
        lo, hi = up[p], up[p + 1]
        if hi > lo:
            last = min(len(groups), (hi + jl - 1) // jl)
            for h in range(n // CHUNK):
                rows = [] if kept[h] is None else [kept[h]]
                rows += pack_run(done, last, h)
                row = jnp.concatenate(rows, axis=1) if len(rows) > 1 else rows[0]
                if row.shape[1] < hi - lo:
                    row = jnp.concatenate([row, jnp.zeros((row.shape[0], hi - lo - row.shape[1]), BF16)], axis=1)
                send1[h * CHUNK : (h + 1) * CHUNK, :, lo:hi] = row[:, : hi - lo].reshape(CHUNK, 16, hi - lo)
                kept[h] = row[:, hi - lo :] if row.shape[1] > hi - lo else None
            done = last
            if p == 0:
                pl.semaphore_wait(barrier, n)
            start_all(copy1, p)
            recv1[me, :, lo:hi] = send1[me, :, lo:hi]

    for load in loads[3:12]:
        load.wait()

    hr = iota((16, nlat), 0)
    lim = lim_ref[...][None, :]
    lim_rows = jnp.where(hr == 0, lim // 8, jnp.where(hr == 1, lim % 8, 0)).astype(F32).astype(BF16)
    hot[...] = onehot(iota((nlat, nlat), 0) == lat_ref[...][None, :])
    got = dot(lim_rows, hot[...])
    row_limit = got[0:1] * 8.0 + got[1:2]
    a = pid_ref[me]
    wave = jnp.where(hr < 8, a, MMAX - 1 - a).astype(F32)
    keep = onehot(wave < row_limit, F32)
    keep_b = keep.astype(BF16)

    r = iota((1, nr), 1)
    first_pad = (MMAX - a + BLOCK - 1) // BLOCK * BLOCK
    first = r < first_pad
    used = (first & (r < MMAX - a)) | ((r >= first_pad) & (r - first_pad <= a))
    degree = jnp.where(first, a + r, MMAX - 1 - a + r - first_pad).astype(F32)
    lam = degree * (degree + 1.0) / float(MMAX * (MMAX - 1))

    levels = nlev * lev_n
    half = (levels + 15) // 16 * 16
    td = ends[1] * K
    mode = onehot(iota((half, levels), 0) == iota((half, levels), 1), F32)
    mode_t = onehot(iota((levels, half), 0) == iota((levels, half), 1), F32)
    own = lev_n * lev
    li, si = iota((levels, td), 0), iota((levels, td), 1)
    pick_div = onehot((li == own + si) & (si < lev_n), F32)
    pick_heat = onehot((li == own + si - lev_n) & (si >= lev_n) & (si < 2 * lev_n), F32)
    si, li = iota((td, levels), 0), iota((td, levels), 1)
    pick_div_t = onehot((li == own + si) & (si < lev_n), F32)
    pick_heat_t = onehot((li == own + si - lev_n) & (si >= lev_n) & (si < 2 * lev_n), F32)
    m_in = mi_ref[...]
    w1 = jnp.concatenate(
        [fdot(fdot(mode, m_in), pick_div), fdot(fdot(mode, fdot(m_in, g_ref[...])), pick_heat)], axis=0
    )
    w2 = fdot(fdot(pick_div_t, mo_ref[...]), mode_t) - 2.0 * fdot(fdot(pick_heat_t, mh_ref[...]), mode_t)
    rates = jnp.sum(
        jnp.where(iota((half, levels), 0) == iota((half, levels), 1), rates_ref[...][None, :], 0.0),
        axis=1, keepdims=True,
    )
    si = iota((td, 1), 0)
    stays = onehot(si >= lev_n, F32)

    def old_rows(p):
        slots = [s for g in groups[ends[p] : ends[p + 1]] for s in g]
        rows = (ends[p + 1] - ends[p]) * K
        total = None
        for c in range(2):
            if not any(s[2] == c for s in slots):
                continue
            row, col = iota((rows, 3 * lev_n), 0), iota((rows, 3 * lev_n), 1)
            src = jnp.full(row.shape, -1, jnp.int32)
            start = 0
            while start < len(slots):
                f, l, cc = slots[start]
                stop = start
                while stop < len(slots) and slots[stop] == (f, l + stop - start, cc):
                    stop += 1
                if cc == c:
                    src = jnp.where((row >= start) & (row < stop), row - start + f * lev_n + l, src)
                start = stop
            part = dot(onehot(col == src), old_all[:, c * nr : (c + 1) * nr])
            total = part if total is None else total + part
        return total

    old_all = jnp.concatenate([old_ref[f, 0] for f in range(3)], axis=0)
    olds = [old_rows(p) for p in range(3)]
    loads[12].wait()

    def forward(p):
        g_n = ends[p + 1] - ends[p]
        cols = jnp.concatenate(
            [
                jnp.concatenate([recv1[d, :, g * jl : (g + 1) * jl] for d in range(n)], axis=1) * keep_b
                for g in range(ends[p], ends[p + 1])
            ],
            axis=0,
        )
        both = lax.dot_general(cols, leg[...], NT, preferred_element_type=F32).reshape(g_n, 2, K, nr)
        total = jnp.where(iota((g_n, K, nr), 2) < first_pad, both[:, 0], both[:, 1]).reshape(g_n * K, nr)
        return jnp.where(used, olds[p] + total, 0.0)

    def inverse(p, new):
        g_n = ends[p + 1] - ends[p]
        sides = jnp.stack(
            [
                jnp.where(first, new, 0.0).reshape(g_n, K, nr),
                jnp.where(first, 0.0, new).reshape(g_n, K, nr),
            ],
            axis=1,
        ).reshape(g_n * 16, nr).astype(BF16)
        out = dot(sides, leg[...])
        return [(out[i * 16 : (i + 1) * 16] * keep).astype(BF16) for i in range(g_n)]

    def exchange(p):
        return pltpu.make_async_remote_copy(
            src_ref=es.at[p], dst_ref=er.at[p], send_sem=es_sem.at[p], recv_sem=er_sem.at[p],
            device_id=(me, other), device_id_type=MESH,
        )

    grids = []

    def send_piece(p):
        lo, hi = down[p], down[p + 1]
        if hi == lo:
            return
        for d in range(n):
            parts, at = [], lo
            while at < hi:
                g = at // jl
                if g >= len(grids):
                    parts.append(jnp.zeros((16, hi - at), BF16))
                    break
                stop = min(hi, (g + 1) * jl)
                parts.append(grids[g][:, d * jl + at - g * jl : d * jl + stop - g * jl])
                at = stop
            send2[d, :, lo:hi] = jnp.concatenate(parts, axis=1) if len(parts) > 1 else parts[0]
        start_all(copy2, p)

    news = []
    for p in range(3):
        if up[p + 1] > up[p]:
            whole(send1, recv1, up, s1, r1, p).wait_recv()
        total = forward(p)
        if p < 2:
            w1s, ts = split3(w1, total)
            res = dot(w1s, ts)
            proj = res[:half] + 2.0 * lam * res[half:]
            es[p] = proj.astype(BF16)
            exchange(p).start()
            exchange(p).wait()
            modal = (proj + er[p].astype(F32)) / (1.0 + 4.0 * lam * rates)
            w2s, ms = split3(w2, modal)
            total = jnp.where(used, total * stays + dot(w2s, ms), 0.0)
        grids += inverse(p, total)
        news.append(total)
        send_piece(p)

    own_copy = pltpu.make_async_copy(send2.at[me], recv2.at[me], out_sem.at[0])
    own_copy.start()

    flat = [s for g in groups for s in g]
    starts = [e * K for e in ends]

    def row_of(slot):
        i = flat.index(slot)
        p = max(j for j in range(3) if starts[j] <= i)
        return p, i - starts[p]

    for c in range(2):
        for f in range(3):
            parts, l = [], 0
            while l < lev_n:
                p, i = row_of((f, l, c))
                stop = l
                while stop < lev_n and row_of((f, stop, c)) == (p, i + stop - l):
                    stop += 1
                parts.append(news[p][i : i + stop - l])
                l = stop
            rows = jnp.concatenate(parts, axis=0) if len(parts) > 1 else parts[0]
            spec_ref[f, 0, :, c * nr : (c + 1) * nr] = rows.astype(BF16)
    spec_copy = pltpu.make_async_copy(spec_ref, spec_hbm, out_sem.at[1])
    spec_copy.start()

    for p in range(3):
        if up[p + 1] > up[p]:
            whole(send1, recv1, up, s1, r1, p).wait_send()
        if down[p + 1] > down[p]:
            whole(send2, recv2, down, s2, r2, p).wait_send()
    own_copy.wait()
    spec_copy.wait()
    for p in range(3):
        if down[p + 1] > down[p]:
            whole(send2, recv2, down, s2, r2, p).wait_recv()


def finish(n, lev_n, jl, got_hbm, spec_in, spec_hbm, out_hbm, got, out_ref, got_sem, sem):
    groups, ends, lanes, up, down = make_pieces(lev_n, jl)
    spec_copy = pltpu.make_async_copy(spec_in, spec_hbm, sem.at[3])
    load = pltpu.make_async_copy(got_hbm, got, got_sem)
    load.start()
    spec_copy.start()
    load.wait()
    where = {s: (g, k) for g, slots in enumerate(groups) for k, s in enumerate(slots)}
    pr, pc = iota((4 * CHUNK * K, 2 * CHUNK * 16), 0), iota((4 * CHUNK * K, 2 * CHUNK * 16), 1)
    q = pr % (4 * CHUNK)
    perm = onehot(pc == q % 2 * (CHUNK * 16) + q // 4 * 16 + q // 2 % 2 * 8 + pr // (4 * CHUNK))
    paired, single = [], {}
    for g, slots in enumerate(groups):
        partners = {where[(f, l, 1)] for f, l, c in slots if c == 0}
        if all(c == 0 for f, l, c in slots) and len({b for b, k in partners}) == 1:
            b = next(iter(partners))[0]
            if all(where[(f, l, 1)] == (b, k) for k, (f, l, c) in enumerate(slots)):
                paired.append((g, b))
    covered = {g for pair in paired for g in pair}
    for g, slots in enumerate(groups):
        if g not in covered:
            single[g] = slots
    for h in range(n // CHUNK):
        rows = got[h * CHUNK : (h + 1) * CHUNK].reshape(CHUNK * 16, lanes)
        qs = slice(h * 4 * CHUNK, (h + 1) * 4 * CHUNK)
        tops = jnp.concatenate([rows[:, g * jl : (g + 1) * jl] for g, b in paired], axis=1)
        bots = jnp.concatenate([rows[:, b * jl : (b + 1) * jl] for g, b in paired], axis=1)
        back = dot(perm, jnp.concatenate([tops, bots], axis=0)).astype(BF16)
        for i, (g, b) in enumerate(paired):
            for k, (f, l, c) in enumerate(groups[g]):
                out_ref[f, l, qs] = back[k * 4 * CHUNK : (k + 1) * 4 * CHUNK, i * jl : (i + 1) * jl]
        for g, slots in single.items():
            zero = [(f, l) for f, l, c in slots if c == 0]
            count = len(zero)
            sr, sc = iota((4 * CHUNK * count, CHUNK * 16), 0), iota((4 * CHUNK * count, CHUNK * 16), 1)
            sq, sk = sr % (4 * CHUNK), sr // (4 * CHUNK)
            some = onehot(sc == sq // 4 * 16 + sq // 2 % 2 * 8 + sk + count * (sq % 2))
            back = dot(some, rows[:, g * jl : (g + 1) * jl]).astype(BF16)
            for k, (f, l) in enumerate(zero):
                out_ref[f, l, qs] = back[k * 4 * CHUNK : (k + 1) * 4 * CHUNK]
    copies = [pltpu.make_async_copy(out_ref.at[f], out_hbm.at[f], sem.at[f]) for f in range(3)]
    for copy in copies:
        copy.start()
    for copy in copies:
        copy.wait()
    spec_copy.wait()


def body(
    fourier_in, spectral_old, legendre, g_matrix, modes_in, modes_out, mode_heating, mode_rates, pair_ids, lat_ids,
    limits,
):
    n, nlev = lax.axis_size("wave"), lax.axis_size("lev")
    fields, lev_n, jl, q_n = fourier_in.shape
    groups, ends, lanes, up, down = make_pieces(lev_n, jl)
    nr, nlat = legendre.shape[1:]
    half = (nlev * lev_n + 15) // 16 * 16
    hbm = pl.BlockSpec(memory_space=pltpu.HBM)
    spec, got = pl.pallas_call(
        functools.partial(kernel, n, nlev),
        out_shape=(
            jax.ShapeDtypeStruct((fields, 1, lev_n, 2 * nr), BF16),
            jax.ShapeDtypeStruct((n, 16, lanes), BF16),
        ),
        in_specs=[hbm] * 11,
        out_specs=(hbm, hbm),
        scratch_shapes=[
            pltpu.VMEM((fields, 1, lev_n, 2 * nr), BF16),
            pltpu.VMEM((fields, lev_n, q_n, jl), BF16),
            pltpu.VMEM((fields, 1, lev_n, 2 * nr), BF16),
            pltpu.VMEM((nr, nlat), BF16),
            pltpu.VMEM(g_matrix.shape, F32),
            pltpu.VMEM(g_matrix.shape, F32),
            pltpu.VMEM(g_matrix.shape, F32),
            pltpu.VMEM(g_matrix.shape, F32),
            pltpu.VMEM(mode_rates.shape, F32),
            pltpu.SMEM(pair_ids.shape, jnp.int32),
            pltpu.VMEM(lat_ids.shape, jnp.int32),
            pltpu.VMEM(limits.shape, jnp.int32),
            pltpu.VMEM((n, 16, lanes), BF16),
            pltpu.VMEM((n, 16, lanes), BF16),
            pltpu.VMEM((n, 16, lanes), BF16),
            pltpu.VMEM((2, half, nr), BF16),
            pltpu.VMEM((2, half, nr), BF16),
            pltpu.VMEM((nlat, nlat), BF16),
            pltpu.SemaphoreType.DMA((2,)),
            pltpu.SemaphoreType.DMA((13,)),
            pltpu.SemaphoreType.DMA((3,)),
            pltpu.SemaphoreType.DMA((3,)),
            pltpu.SemaphoreType.DMA((3,)),
            pltpu.SemaphoreType.DMA((3,)),
            pltpu.SemaphoreType.DMA((2,)),
            pltpu.SemaphoreType.DMA((2,)),
        ],
        compiler_params=pltpu.CompilerParams(
            collective_id=0, has_side_effects=True, vmem_limit_bytes=48 * 1024 * 1024
        ),
        cost_estimate=pl.CostEstimate(flops=10**9, bytes_accessed=8 * 10**6, transcendentals=0),
    )(
        *[
            pltpu.with_memory_space_constraint(x, pltpu.HBM)
            for x in (
                jnp.transpose(fourier_in, (0, 1, 3, 2)),
                jnp.transpose(spectral_old, (0, 2, 1, 3)),
                legendre,
                g_matrix,
                modes_in,
                modes_out,
                mode_heating,
                mode_rates,
                pair_ids,
                lat_ids,
                limits,
            )
        ]
    )
    spec, out = pl.pallas_call(
        functools.partial(finish, n, lev_n, jl),
        out_shape=(
            jax.ShapeDtypeStruct((fields, 1, lev_n, 2 * nr), BF16),
            jax.ShapeDtypeStruct((fields, lev_n, q_n, jl), BF16),
        ),
        in_specs=[hbm] * 2,
        out_specs=(hbm, hbm),
        scratch_shapes=[
            pltpu.VMEM((n, 16, lanes), BF16),
            pltpu.VMEM((fields, lev_n, q_n, jl), BF16),
            pltpu.SemaphoreType.DMA,
            pltpu.SemaphoreType.DMA((4,)),
        ],
        compiler_params=pltpu.CompilerParams(vmem_limit_bytes=48 * 1024 * 1024),
        cost_estimate=pl.CostEstimate(flops=2 * 10**8, bytes_accessed=2 * 10**6, transcendentals=0),
    )(got, spec)
    return jnp.transpose(spec, (0, 2, 1, 3)), jnp.transpose(out, (0, 1, 3, 2))


def solution(mesh):
    wave = P(None, "lev", "wave", None)
    return jax.shard_map(
        body,
        mesh=mesh,
        in_specs=(wave, wave, P("wave", None, None)) + (P(),) * 8,
        out_specs=(wave, wave),
        check_vma=False,
    )
```

```python
import functools

import jax
import jax.numpy as jnp
from jax import lax
from jax.experimental import pallas as pl
from jax.experimental.pallas import tpu as pltpu
from jax.sharding import PartitionSpec as P

MMAX = 1280
BLOCK = 64
K = 8
CHUNK = 16
F32, BF16 = jnp.float32, jnp.bfloat16
MESH = pl.DeviceIdType.MESH
HI = lax.Precision.HIGHEST
NT = (((1,), (1,)), ((), ()))


def iota(shape, dim):
    return lax.broadcasted_iota(jnp.int32, shape, dim)


def dot(a, b):
    return jnp.dot(a, b, preferred_element_type=F32)


def fdot(a, b):
    return jnp.dot(a, b, precision=HI, preferred_element_type=F32)


def onehot(mask, dtype=BF16):
    return jnp.where(mask, 1.0, 0.0).astype(dtype)


def split3(left, right):
    lh = left.astype(BF16)
    ll = (left - lh.astype(F32)).astype(BF16)
    rh = right.astype(BF16)
    rl = (right - rh.astype(F32)).astype(BF16)
    return jnp.concatenate([lh, lh, ll], axis=1), jnp.concatenate([rh, rl, rh], axis=0)


def make_slots(lev_n):
    fill = -2 * lev_n % K
    rest = list(range(fill, lev_n))
    whole = len(rest) // K * K
    slots = []
    for levels in (rest[:whole], rest[whole:]):
        for c in range(2):
            slots += [(0, l, c) for l in levels]
    groups = [slots[i : i + K] for i in range(0, len(slots), K)]
    ends = [0, len(groups)]
    for c in range(2):
        slots = [(f, l, c) for f in (1, 2) for l in range(lev_n)] + [(0, l, c) for l in range(fill)]
        groups += [slots[i : i + K] for i in range(0, len(slots), K)]
        ends.append(len(groups))
    return groups, ends


def make_pieces(lev_n, jl):
    groups, ends = make_slots(lev_n)
    count = len(groups)
    lanes = (count * jl + 127) // 128 * 128
    pad = -ends[1] * jl % 128
    if count * jl + pad > lanes:
        pad = 0
    first = [g * jl + (pad if g >= ends[1] else 0) for g in range(count)] + [lanes]
    stops = [first[ends[1]], first[ends[2]], lanes]
    up = [min((e + 127) // 128 * 128, lanes) for e in stops]
    down = [e // 128 * 128 for e in stops]
    return groups, ends, lanes, first, [0] + up, [0] + down


def lane_parts(first, jl, lo, hi):
    parts, at = [], lo
    while at < hi:
        g = max(i for i in range(len(first) - 1) if first[i] <= at)
        if at < first[g] + jl:
            stop = min(hi, first[g] + jl)
            parts.append((g, at - first[g], stop - first[g]))
        else:
            stop = min(hi, first[g + 1])
            parts.append((None, 0, stop - at))
        at = stop
    return parts


def kernel(
    n, nlev, x_hbm, old_hbm, leg_hbm, g_hbm, mi_hbm, mo_hbm, mh_hbm, rates_hbm, pid_hbm, lat_hbm, lim_hbm,
    spec_hbm, recv2,
    spec_ref, x_ref, old_ref, leg, g_ref, mi_ref, mo_ref, mh_ref, rates_ref, pid_ref, lat_ref, lim_ref,
    send1, recv1, send2, es, er, hot, turned,
    out_sem, in_sem, s1, r1, s2, r2, es_sem, er_sem,
):
    lev_n = x_ref.shape[1]
    jl = x_ref.shape[3]
    groups, ends, lanes, base, up, down = make_pieces(lev_n, jl)
    nr, nlat = leg_hbm.shape[1:]
    me, lev = lax.axis_index("wave"), lax.axis_index("lev")
    other = lax.rem(lev + 1, nlev)
    plane = n // 4
    z, xy = me // plane, lax.rem(me, plane)
    low = z < 2

    def target(i):
        zi, k = i // plane, lax.rem(i, plane)
        far = jnp.where(low, 3 - zi, zi)
        near = jnp.where(zi == 2, z + 1 - 2 * lax.rem(z, 2), z)
        tz = jnp.where(zi < 2, far, near)
        return tz * plane + lax.rem(xy + k + zi // 3, plane)

    pairs = [(x_hbm.at[f], x_ref.at[f]) for f in (0, 1, 2)] + [
        (pid_hbm, pid_ref), (lat_hbm, lat_ref), (lim_hbm, lim_ref), (g_hbm, g_ref), (mi_hbm, mi_ref),
        (mo_hbm, mo_ref), (mh_hbm, mh_ref), (rates_hbm, rates_ref), (old_hbm, old_ref), (leg_hbm.at[0], leg),
    ]
    loads = [pltpu.make_async_copy(src, dst, in_sem.at[i]) for i, (src, dst) in enumerate(pairs)]
    for load in loads[:3]:
        load.start()
    barrier = pltpu.get_barrier_semaphore()

    def greet(i, carry):
        pl.semaphore_signal(barrier, inc=1, device_id=(target(i), lev), device_id_type=MESH)
        return carry

    lax.fori_loop(0, n - 1, greet, 0)
    pl.semaphore_signal(barrier, inc=1, device_id=(me, other), device_id_type=MESH)
    for load in loads[3:]:
        load.start()

    pr, pc = iota((CHUNK * 16, 4 * CHUNK * K), 0), iota((CHUNK * 16, 4 * CHUNK * K), 1)
    home = pr % K * (4 * CHUNK) + pr // 16 * 4 + pr // 8 % 2 * 2

    def perm_of(g):
        part = jnp.zeros(pr.shape, jnp.int32)
        for k, (f, l, c) in enumerate(groups[g]):
            if c:
                part = jnp.where(pr % K == k, 1, part)
        return onehot(pc == home + part)

    def parts_of(g):
        return tuple(c for f, l, c in groups[g])

    perms = {}
    for g in range(len(groups)):
        if parts_of(g) not in perms:
            perms[parts_of(g)] = perm_of(g)

    def packed(g, h):
        blocks = [x_ref[f, l, h * 4 * CHUNK : (h + 1) * 4 * CHUNK] for f, l, c in groups[g]]
        blocks += [jnp.zeros_like(blocks[0])] * (K - len(blocks))
        return jnp.concatenate(blocks, axis=0)

    def pack_run(first, last, h):
        out, g = [], first
        while g < last:
            run = [g]
            while run[-1] + 1 < last and parts_of(run[-1] + 1) == parts_of(g):
                run.append(run[-1] + 1)
            data = [packed(i, h) for i in run]
            data = jnp.concatenate(data, axis=1) if len(run) > 1 else data[0]
            data = dot(perms[parts_of(g)], data).astype(BF16)
            out += [data[:, i * jl : (i + 1) * jl] for i in range(len(run))]
            g = run[-1] + 1
        return out

    def copy1(p, to):
        at = pl.ds(up[p], up[p + 1] - up[p])
        return pltpu.make_async_remote_copy(
            src_ref=send1.at[to, :, at], dst_ref=recv1.at[me, :, at], send_sem=s1.at[p], recv_sem=r1.at[p],
            device_id=(to, lev), device_id_type=MESH,
        )

    def copy2(p, to):
        at = pl.ds(down[p], down[p + 1] - down[p])
        return pltpu.make_async_remote_copy(
            src_ref=send2.at[to, :, at], dst_ref=recv2.at[me, :, at], send_sem=s2.at[p], recv_sem=r2.at[p],
            device_id=(to, lev), device_id_type=MESH,
        )

    def start_all(copy, p):
        def start(i, carry):
            copy(p, target(i)).start()
            return carry

        def start_up(i, carry):
            copy(p, jnp.where(i < me, i, i + 1)).start()
            return carry

        lax.fori_loop(0, n - 1, start_up if copy is copy2 else start, 0)

    def whole(src, dst, bounds, ss, rr, p):
        at = pl.ds(bounds[p], bounds[p + 1] - bounds[p])
        return pltpu.make_async_remote_copy(
            src_ref=src.at[pl.ds(0, n - 1), :, at], dst_ref=dst.at[pl.ds(0, n - 1), :, at], send_sem=ss.at[p],
            recv_sem=rr.at[p], device_id=(me, other), device_id_type=MESH,
        )

    done = 0
    held = {}
    for p in range(3):
        lo, hi = up[p], up[p + 1]
        if p == 0:
            loads[0].wait()
        if p == 1:
            loads[1].wait()
            loads[2].wait()
        if hi == lo:
            continue
        parts = lane_parts(base, jl, lo, hi)
        last = max([g + 1 for g, u, v in parts if g is not None] + [done])
        for h in range(n // CHUNK):
            held.update({(h, done + i): x for i, x in enumerate(pack_run(done, last, h))})
            row = [
                jnp.zeros((CHUNK * 16, v), BF16) if g is None else held[h, g][:, u:v] for g, u, v in parts
            ]
            row = jnp.concatenate(row, axis=1) if len(row) > 1 else row[0]
            send1[h * CHUNK : (h + 1) * CHUNK, :, lo:hi] = row.reshape(CHUNK, 16, hi - lo)
        done = last
        if p == 0:
            pl.semaphore_wait(barrier, n)
        start_all(copy1, p)
        recv1[me, :, lo:hi] = send1[me, :, lo:hi]

    for load in loads[3:12]:
        load.wait()

    hr = iota((16, nlat), 0)
    lim = lim_ref[...][None, :]
    lim_rows = jnp.where(hr == 0, lim // 8, jnp.where(hr == 1, lim % 8, 0)).astype(F32).astype(BF16)
    hot[...] = onehot(iota((nlat, nlat), 0) == lat_ref[...][None, :])
    got = dot(lim_rows, hot[...])
    row_limit = got[0:1] * 8.0 + got[1:2]
    a = pid_ref[me]
    wave = jnp.where(hr < 8, a, MMAX - 1 - a).astype(F32)
    keep = onehot(wave < row_limit, F32)
    keep_b = keep.astype(BF16)

    r = iota((1, nr), 1)
    first_pad = (MMAX - a + BLOCK - 1) // BLOCK * BLOCK
    first = r < first_pad
    used = (first & (r < MMAX - a)) | ((r >= first_pad) & (r - first_pad <= a))
    degree = jnp.where(first, a + r, MMAX - 1 - a + r - first_pad).astype(F32)
    lam = degree * (degree + 1.0) / float(MMAX * (MMAX - 1))

    levels = nlev * lev_n
    half = (levels + 15) // 16 * 16
    td = (ends[2] - ends[1]) * K
    mode = onehot(iota((half, levels), 0) == iota((half, levels), 1), F32)
    mode_t = onehot(iota((levels, half), 0) == iota((levels, half), 1), F32)
    own = lev_n * lev
    li, si = iota((levels, td), 0), iota((levels, td), 1)
    pick_div = onehot((li == own + si) & (si < lev_n), F32)
    pick_heat = onehot((li == own + si - lev_n) & (si >= lev_n) & (si < 2 * lev_n), F32)
    si, li = iota((td, levels), 0), iota((td, levels), 1)
    pick_div_t = onehot((li == own + si) & (si < lev_n), F32)
    pick_heat_t = onehot((li == own + si - lev_n) & (si >= lev_n) & (si < 2 * lev_n), F32)
    m_in = mi_ref[...]
    w1 = jnp.concatenate(
        [fdot(fdot(mode, m_in), pick_div), fdot(fdot(mode, fdot(m_in, g_ref[...])), pick_heat)], axis=0
    )
    w2 = fdot(fdot(pick_div_t, mo_ref[...]), mode_t) - 2.0 * fdot(fdot(pick_heat_t, mh_ref[...]), mode_t)
    rates = jnp.sum(
        jnp.where(iota((half, levels), 0) == iota((half, levels), 1), rates_ref[...][None, :], 0.0),
        axis=1, keepdims=True,
    )
    si = iota((td, 1), 0)
    stays = onehot(si >= lev_n, F32)

    def old_rows(p):
        slots = [s for g in groups[ends[p] : ends[p + 1]] for s in g]
        rows = (ends[p + 1] - ends[p]) * K
        total = None
        for c in range(2):
            if not any(s[2] == c for s in slots):
                continue
            row, col = iota((rows, 3 * lev_n), 0), iota((rows, 3 * lev_n), 1)
            src = jnp.full(row.shape, -1, jnp.int32)
            start = 0
            while start < len(slots):
                f, l, cc = slots[start]
                stop = start
                while stop < len(slots) and slots[stop] == (f, l + stop - start, cc):
                    stop += 1
                if cc == c:
                    src = jnp.where((row >= start) & (row < stop), row - start + f * lev_n + l, src)
                start = stop
            part = dot(onehot(col == src), old_all[:, c * nr : (c + 1) * nr])
            total = part if total is None else total + part
        return total

    old_all = jnp.concatenate([old_ref[f, 0] for f in range(3)], axis=0)
    olds = [old_rows(p) for p in range(3)]
    loads[12].wait()

    def turn(i, carry):
        at = pl.ds(pl.multiple_of(i * 128, 128), 128)
        turned[:, at] = leg[at, :].T
        return carry

    lax.fori_loop(0, nr // 128, turn, 0)

    def forward(p):
        g_n = ends[p + 1] - ends[p]
        cols = jnp.concatenate(
            [
                jnp.concatenate([recv1[d, :, base[g] : base[g] + jl] for d in range(n)], axis=1) * keep_b
                for g in range(ends[p], ends[p + 1])
            ],
            axis=0,
        )
        both = dot(cols, turned[...]).reshape(g_n, 2, K, nr)
        total = jnp.where(iota((g_n, K, nr), 2) < first_pad, both[:, 0], both[:, 1]).reshape(g_n * K, nr)
        return jnp.where(used, olds[p] + total, 0.0)

    def inverse(p, new):
        g_n = ends[p + 1] - ends[p]
        sides = jnp.stack(
            [
                jnp.where(first, new, 0.0).reshape(g_n, K, nr),
                jnp.where(first, 0.0, new).reshape(g_n, K, nr),
            ],
            axis=1,
        ).reshape(g_n * 16, nr).astype(BF16)
        out = dot(sides, leg[...])
        return [(out[i * 16 : (i + 1) * 16] * keep).astype(BF16) for i in range(g_n)]

    def exchange(p):
        return pltpu.make_async_remote_copy(
            src_ref=es.at[p], dst_ref=er.at[p], send_sem=es_sem.at[p], recv_sem=er_sem.at[p],
            device_id=(me, other), device_id_type=MESH,
        )

    grids = []

    def fill_piece(p):
        lo, hi = down[p], down[p + 1]
        for d in range(n if hi > lo else 0):
            row = [
                jnp.zeros((16, v), BF16) if g is None else grids[g][:, d * jl + u : d * jl + v]
                for g, u, v in lane_parts(base, jl, lo, hi)
            ]
            send2[d, :, lo:hi] = jnp.concatenate(row, axis=1) if len(row) > 1 else row[0]

    def send_piece(p):
        if down[p + 1] > down[p]:
            start_all(copy2, p)

    def arrive(p):
        if up[p + 1] > up[p]:
            whole(send1, recv1, up, s1, r1, p).wait_recv()

    def project(p, total):
        w1s, ts = split3(w1, total)
        res = dot(w1s, ts)
        proj = res[:half] + 2.0 * lam * res[half:]
        es[p - 1] = proj.astype(BF16)
        exchange(p - 1).start()
        return proj

    def step(p, total, proj):
        exchange(p - 1).wait()
        modal = (proj + er[p - 1].astype(F32)) / (1.0 + 4.0 * lam * rates)
        w2s, ms = split3(w2, modal)
        return jnp.where(used, total * stays + dot(w2s, ms), 0.0)

    arrive(0)
    vort = forward(0)
    grids += inverse(0, vort)
    fill_piece(0)
    arrive(1)
    total1 = forward(1)
    proj1 = project(1, total1)
    send_piece(0)
    arrive(2)
    total2 = forward(2)
    proj2 = project(2, total2)
    new1 = step(1, total1, proj1)
    grids += inverse(1, new1)
    fill_piece(1)
    send_piece(1)
    new2 = step(2, total2, proj2)
    grids += inverse(2, new2)
    fill_piece(2)
    send_piece(2)
    news = [vort, new1, new2]

    own_copy = pltpu.make_async_copy(send2.at[me], recv2.at[me], out_sem.at[0])
    own_copy.start()

    flat = [s for g in groups for s in g + [None] * (K - len(g))]
    starts = [e * K for e in ends]

    def row_of(slot):
        i = flat.index(slot)
        p = max(j for j in range(3) if starts[j] <= i)
        return p, i - starts[p]

    for c in range(2):
        for f in range(3):
            parts, l = [], 0
            while l < lev_n:
                p, i = row_of((f, l, c))
                stop = l
                while stop < lev_n and row_of((f, stop, c)) == (p, i + stop - l):
                    stop += 1
                parts.append(news[p][i : i + stop - l])
                l = stop
            rows = jnp.concatenate(parts, axis=0) if len(parts) > 1 else parts[0]
            spec_ref[f, 0, :, c * nr : (c + 1) * nr] = rows.astype(BF16)
    spec_copy = pltpu.make_async_copy(spec_ref, spec_hbm, out_sem.at[1])
    spec_copy.start()

    for p in range(3):
        if up[p + 1] > up[p]:
            whole(send1, recv1, up, s1, r1, p).wait_send()
        if down[p + 1] > down[p]:
            whole(send2, recv2, down, s2, r2, p).wait_send()
    own_copy.wait()
    spec_copy.wait()
    for p in range(3):
        if down[p + 1] > down[p]:
            whole(send2, recv2, down, s2, r2, p).wait_recv()


def finish(n, lev_n, jl, got, spec_in, spec_hbm, out_hbm, out_ref, sem):
    groups, ends, lanes, base, up, down = make_pieces(lev_n, jl)
    spec_copy = pltpu.make_async_copy(spec_in, spec_hbm, sem.at[3])
    spec_copy.start()
    where = {s: (g, k) for g, slots in enumerate(groups) for k, s in enumerate(slots)}
    pr, pc = iota((4 * CHUNK * K, 2 * CHUNK * 16), 0), iota((4 * CHUNK * K, 2 * CHUNK * 16), 1)
    q = pr % (4 * CHUNK)
    perm = onehot(pc == q % 2 * (CHUNK * 16) + q // 4 * 16 + q // 2 % 2 * 8 + pr // (4 * CHUNK))
    paired, single = [], {}
    for g, slots in enumerate(groups):
        partners = {where[(f, l, 1)] for f, l, c in slots if c == 0}
        if all(c == 0 for f, l, c in slots) and len({b for b, k in partners}) == 1:
            b = next(iter(partners))[0]
            if all(where[(f, l, 1)] == (b, k) for k, (f, l, c) in enumerate(slots)):
                paired.append((g, b))
    covered = {g for pair in paired for g in pair}
    for g, slots in enumerate(groups):
        if g not in covered:
            single[g] = slots
    for h in range(n // CHUNK):
        rows = got[h * CHUNK : (h + 1) * CHUNK].reshape(CHUNK * 16, lanes)
        qs = slice(h * 4 * CHUNK, (h + 1) * 4 * CHUNK)
        tops = jnp.concatenate([rows[:, base[g] : base[g] + jl] for g, b in paired], axis=1)
        bots = jnp.concatenate([rows[:, base[b] : base[b] + jl] for g, b in paired], axis=1)
        back = dot(perm, jnp.concatenate([tops, bots], axis=0)).astype(BF16)
        for i, (g, b) in enumerate(paired):
            for k, (f, l, c) in enumerate(groups[g]):
                out_ref[f, l, qs] = back[k * 4 * CHUNK : (k + 1) * 4 * CHUNK, i * jl : (i + 1) * jl]
        for g, slots in single.items():
            zero = [(f, l) for f, l, c in slots if c == 0]
            count = len(zero)
            sr, sc = iota((4 * CHUNK * count, CHUNK * 16), 0), iota((4 * CHUNK * count, CHUNK * 16), 1)
            sq, sk = sr % (4 * CHUNK), sr // (4 * CHUNK)
            some = onehot(sc == sq // 4 * 16 + sq // 2 % 2 * 8 + sk + count * (sq % 2))
            back = dot(some, rows[:, base[g] : base[g] + jl]).astype(BF16)
            for k, (f, l) in enumerate(zero):
                out_ref[f, l, qs] = back[k * 4 * CHUNK : (k + 1) * 4 * CHUNK]
    copies = [pltpu.make_async_copy(out_ref.at[f], out_hbm.at[f], sem.at[f]) for f in range(3)]
    for copy in copies:
        copy.start()
    for copy in copies:
        copy.wait()
    spec_copy.wait()


def body(
    fourier_in, spectral_old, legendre, g_matrix, modes_in, modes_out, mode_heating, mode_rates, pair_ids, lat_ids,
    limits,
):
    n, nlev = lax.axis_size("wave"), lax.axis_size("lev")
    fields, lev_n, jl, q_n = fourier_in.shape
    groups, ends, lanes, base, up, down = make_pieces(lev_n, jl)
    nr, nlat = legendre.shape[1:]
    half = (nlev * lev_n + 15) // 16 * 16
    hbm = pl.BlockSpec(memory_space=pltpu.HBM)
    spec, got = pl.pallas_call(
        functools.partial(kernel, n, nlev),
        out_shape=(
            jax.ShapeDtypeStruct((fields, 1, lev_n, 2 * nr), BF16),
            jax.ShapeDtypeStruct((n, 16, lanes), BF16),
        ),
        in_specs=[hbm] * 11,
        out_specs=(hbm, hbm),
        scratch_shapes=[
            pltpu.VMEM((fields, 1, lev_n, 2 * nr), BF16),
            pltpu.VMEM((fields, lev_n, q_n, jl), BF16),
            pltpu.VMEM((fields, 1, lev_n, 2 * nr), BF16),
            pltpu.VMEM((nr, nlat), BF16),
            pltpu.VMEM(g_matrix.shape, F32),
            pltpu.VMEM(g_matrix.shape, F32),
            pltpu.VMEM(g_matrix.shape, F32),
            pltpu.VMEM(g_matrix.shape, F32),
            pltpu.VMEM(mode_rates.shape, F32),
            pltpu.SMEM(pair_ids.shape, jnp.int32),
            pltpu.VMEM(lat_ids.shape, jnp.int32),
            pltpu.VMEM(limits.shape, jnp.int32),
            pltpu.VMEM((n, 16, lanes), BF16),
            pltpu.VMEM((n, 16, lanes), BF16),
            pltpu.VMEM((n, 16, lanes), BF16),
            pltpu.VMEM((2, half, nr), BF16),
            pltpu.VMEM((2, half, nr), BF16),
            pltpu.VMEM((nlat, nlat), BF16),
            pltpu.VMEM((nlat, nr), BF16),
            pltpu.SemaphoreType.DMA((2,)),
            pltpu.SemaphoreType.DMA((13,)),
            pltpu.SemaphoreType.DMA((3,)),
            pltpu.SemaphoreType.DMA((3,)),
            pltpu.SemaphoreType.DMA((3,)),
            pltpu.SemaphoreType.DMA((3,)),
            pltpu.SemaphoreType.DMA((2,)),
            pltpu.SemaphoreType.DMA((2,)),
        ],
        compiler_params=pltpu.CompilerParams(
            collective_id=0, has_side_effects=True, vmem_limit_bytes=48 * 1024 * 1024
        ),
        cost_estimate=pl.CostEstimate(flops=10**9, bytes_accessed=8 * 10**6, transcendentals=0),
    )(
        *[
            pltpu.with_memory_space_constraint(x, pltpu.HBM)
            for x in (
                jnp.transpose(fourier_in, (0, 1, 3, 2)),
                jnp.transpose(spectral_old, (0, 2, 1, 3)),
                legendre,
                g_matrix,
                modes_in,
                modes_out,
                mode_heating,
                mode_rates,
                pair_ids,
                lat_ids,
                limits,
            )
        ]
    )
    spec, out = pl.pallas_call(
        functools.partial(finish, n, lev_n, jl),
        out_shape=(
            jax.ShapeDtypeStruct((fields, 1, lev_n, 2 * nr), BF16),
            jax.ShapeDtypeStruct((fields, lev_n, q_n, jl), BF16),
        ),
        in_specs=[pl.BlockSpec(memory_space=pltpu.VMEM)] * 2,
        out_specs=(hbm, hbm),
        scratch_shapes=[
            pltpu.VMEM((fields, lev_n, q_n, jl), BF16),
            pltpu.SemaphoreType.DMA((4,)),
        ],
        compiler_params=pltpu.CompilerParams(vmem_limit_bytes=48 * 1024 * 1024),
        cost_estimate=pl.CostEstimate(flops=2 * 10**8, bytes_accessed=2 * 10**6, transcendentals=0),
    )(got, spec)
    return jnp.transpose(spec, (0, 2, 1, 3)), jnp.transpose(out, (0, 1, 3, 2))


def solution(mesh):
    wave = P(None, "lev", "wave", None)
    return jax.shard_map(
        body,
        mesh=mesh,
        in_specs=(wave, wave, P("wave", None, None)) + (P(),) * 8,
        out_specs=(wave, wave),
        check_vma=False,
    )
```

```python
import functools

import jax
import jax.numpy as jnp
from jax import lax
from jax.experimental import pallas as pl
from jax.experimental.pallas import tpu as pltpu
from jax.sharding import PartitionSpec as P

MMAX = 1280
BLOCK = 64
K = 8
CHUNK = 16
F32, BF16 = jnp.float32, jnp.bfloat16
MESH = pl.DeviceIdType.MESH
HI = lax.Precision.HIGHEST
NT = (((1,), (1,)), ((), ()))


def iota(shape, dim):
    return lax.broadcasted_iota(jnp.int32, shape, dim)


def dot(a, b):
    return jnp.dot(a, b, preferred_element_type=F32)


def fdot(a, b):
    return jnp.dot(a, b, precision=HI, preferred_element_type=F32)


def onehot(mask, dtype=BF16):
    return jnp.where(mask, 1.0, 0.0).astype(dtype)


def split3(left, right):
    lh = left.astype(BF16)
    ll = (left - lh.astype(F32)).astype(BF16)
    rh = right.astype(BF16)
    rl = (right - rh.astype(F32)).astype(BF16)
    return jnp.concatenate([lh, lh, ll], axis=1), jnp.concatenate([rh, rl, rh], axis=0)


def make_slots(lev_n):
    fill = -2 * lev_n % K
    rest = list(range(fill, lev_n))
    whole = len(rest) // K * K
    slots = []
    for levels in (rest[:whole], rest[whole:]):
        for c in range(2):
            slots += [(0, l, c) for l in levels]
    groups = [slots[i : i + K] for i in range(0, len(slots), K)]
    ends = [0, len(groups)]
    for c in range(2):
        slots = [(f, l, c) for f in (1, 2) for l in range(lev_n)] + [(0, l, c) for l in range(fill)]
        groups += [slots[i : i + K] for i in range(0, len(slots), K)]
        ends.append(len(groups))
    return groups, ends


def make_pieces(lev_n, jl):
    groups, ends = make_slots(lev_n)
    count = len(groups)
    lanes = (count * jl + 127) // 128 * 128
    pad = -ends[1] * jl % 128
    if count * jl + pad > lanes:
        pad = 0
    first = [g * jl + (pad if g >= ends[1] else 0) for g in range(count)] + [lanes]
    stops = [first[ends[1]], first[ends[2]], lanes]
    up = [min((e + 127) // 128 * 128, lanes) for e in stops]
    down = [e // 128 * 128 for e in stops]
    return groups, ends, lanes, first, [0] + up, [0] + down


def lane_parts(first, jl, lo, hi):
    parts, at = [], lo
    while at < hi:
        g = max(i for i in range(len(first) - 1) if first[i] <= at)
        if at < first[g] + jl:
            stop = min(hi, first[g] + jl)
            parts.append((g, at - first[g], stop - first[g]))
        else:
            stop = min(hi, first[g + 1])
            parts.append((None, 0, stop - at))
        at = stop
    return parts


def kernel(
    n, nlev, x_hbm, old_hbm, leg_hbm, g_hbm, mi_hbm, mo_hbm, mh_hbm, rates_hbm, pid_hbm, lat_hbm, lim_hbm,
    spec_ref, out_ref,
    x_ref, old_ref, leg, g_ref, mi_ref, mo_ref, mh_ref, rates_ref, pid_ref, lat_ref, lim_ref,
    send1, recv1, send2, recv2, es, er, hot, turned,
    in_sem, s1, r1, s2, r2, es_sem, er_sem,
):
    lev_n = x_ref.shape[1]
    jl = x_ref.shape[3]
    groups, ends, lanes, base, up, down = make_pieces(lev_n, jl)
    nr, nlat = leg_hbm.shape[1:]
    me, lev = lax.axis_index("wave"), lax.axis_index("lev")
    other = lax.rem(lev + 1, nlev)

    pairs = [(x_hbm.at[f], x_ref.at[f]) for f in (0, 1, 2)] + [
        (pid_hbm, pid_ref), (lat_hbm, lat_ref), (lim_hbm, lim_ref), (g_hbm, g_ref), (mi_hbm, mi_ref),
        (mo_hbm, mo_ref), (mh_hbm, mh_ref), (rates_hbm, rates_ref), (old_hbm, old_ref), (leg_hbm.at[0], leg),
    ]
    loads = [pltpu.make_async_copy(src, dst, in_sem.at[i]) for i, (src, dst) in enumerate(pairs)]
    for load in loads[:3]:
        load.start()
    def away(i):
        return lax.bitwise_xor(me, n - 1 - i)

    def upwards(i):
        return jnp.where(i < me, i, i + 1)

    barrier = pltpu.get_barrier_semaphore()

    def greet(i, carry):
        pl.semaphore_signal(barrier, inc=1, device_id=(upwards(i), lev), device_id_type=MESH)
        return carry

    lax.fori_loop(0, n - 1, greet, 0)
    pl.semaphore_signal(barrier, inc=1, device_id=(me, other), device_id_type=MESH)
    for load in loads[3:]:
        load.start()

    pr, pc = iota((CHUNK * 16, 1), 0), iota((1, 4 * CHUNK * K), 1)
    home = pr % K * (4 * CHUNK) + pr // 16 * 4 + pr // 8 % 2 * 2

    def perm_of(g):
        part = jnp.zeros(pr.shape, jnp.int32)
        for k, (f, l, c) in enumerate(groups[g]):
            if c:
                part = jnp.where(pr % K == k, 1, part)
        return onehot(pc == home + part)

    def parts_of(g):
        return tuple(c for f, l, c in groups[g])

    perms = {}
    for g in range(len(groups)):
        if parts_of(g) not in perms:
            perms[parts_of(g)] = perm_of(g)

    def packed(g, h):
        blocks = [x_ref[f, l, h * 4 * CHUNK : (h + 1) * 4 * CHUNK] for f, l, c in groups[g]]
        blocks += [jnp.zeros_like(blocks[0])] * (K - len(blocks))
        return jnp.concatenate(blocks, axis=0)

    def pack_run(first, last, h):
        out, g = [], first
        while g < last:
            run = [g]
            while run[-1] + 1 < last and parts_of(run[-1] + 1) == parts_of(g):
                run.append(run[-1] + 1)
            data = [packed(i, h) for i in run]
            data = jnp.concatenate(data, axis=1) if len(run) > 1 else data[0]
            data = dot(perms[parts_of(g)], data).astype(BF16)
            out += [data[:, i * jl : (i + 1) * jl] for i in range(len(run))]
            g = run[-1] + 1
        return out

    def copy1(p, to):
        at = pl.ds(up[p], up[p + 1] - up[p])
        return pltpu.make_async_remote_copy(
            src_ref=send1.at[to, :, at], dst_ref=recv1.at[me, :, at], send_sem=s1.at[p], recv_sem=r1.at[p],
            device_id=(to, lev), device_id_type=MESH,
        )

    def copy2(p, to):
        at = pl.ds(down[p], down[p + 1] - down[p])
        return pltpu.make_async_remote_copy(
            src_ref=send2.at[to, :, at], dst_ref=recv2.at[me, :, at], send_sem=s2.at[p], recv_sem=r2.at[p],
            device_id=(to, lev), device_id_type=MESH,
        )

    def start_all(copy, p, order):
        def start(i, carry):
            copy(p, order(i)).start()
            return carry

        lax.fori_loop(0, n - 1, start, 0)

    def whole(src, dst, bounds, ss, rr, p):
        at = pl.ds(bounds[p], bounds[p + 1] - bounds[p])
        return pltpu.make_async_remote_copy(
            src_ref=src.at[pl.ds(0, n - 1), :, at], dst_ref=dst.at[pl.ds(0, n - 1), :, at], send_sem=ss.at[p],
            recv_sem=rr.at[p], device_id=(me, other), device_id_type=MESH,
        )

    done = 0
    held = {}
    for p in range(3):
        lo, hi = up[p], up[p + 1]
        if p == 0:
            loads[0].wait()
        if p == 1:
            loads[1].wait()
            loads[2].wait()
        if hi == lo:
            continue
        parts = lane_parts(base, jl, lo, hi)
        last = max([g + 1 for g, u, v in parts if g is not None] + [done])
        for h in range(n // CHUNK):
            held.update({(h, done + i): x for i, x in enumerate(pack_run(done, last, h))})
            row = [
                jnp.zeros((CHUNK * 16, v), BF16) if g is None else held[h, g][:, u:v] for g, u, v in parts
            ]
            row = jnp.concatenate(row, axis=1) if len(row) > 1 else row[0]
            send1[h * CHUNK : (h + 1) * CHUNK, :, lo:hi] = row.reshape(CHUNK, 16, hi - lo)
        done = last
        if p == 0:
            pl.semaphore_wait(barrier, n)
        start_all(copy1, p, away)
        recv1[me, :, lo:hi] = send1[me, :, lo:hi]

    for load in loads[3:12]:
        load.wait()

    hr = iota((16, nlat), 0)
    lim = lim_ref[...][None, :]
    lim_rows = jnp.where(hr == 0, lim // 8, jnp.where(hr == 1, lim % 8, 0)).astype(F32).astype(BF16)
    hot[...] = onehot(iota((nlat, nlat), 0) == lat_ref[...][None, :])
    got = dot(lim_rows, hot[...])
    row_limit = got[0:1] * 8.0 + got[1:2]
    a = pid_ref[me]
    wave = jnp.where(hr < 8, a, MMAX - 1 - a).astype(F32)
    keep = onehot(wave < row_limit, F32)
    keep_b = keep.astype(BF16)

    r = iota((1, nr), 1)
    first_pad = (MMAX - a + BLOCK - 1) // BLOCK * BLOCK
    first = r < first_pad
    used = (first & (r < MMAX - a)) | ((r >= first_pad) & (r - first_pad <= a))
    degree = jnp.where(first, a + r, MMAX - 1 - a + r - first_pad).astype(F32)
    lam = degree * (degree + 1.0) / float(MMAX * (MMAX - 1))

    levels = nlev * lev_n
    half = (levels + 15) // 16 * 16
    td = (ends[2] - ends[1]) * K
    mode = onehot(iota((half, levels), 0) == iota((half, levels), 1), F32)
    mode_t = onehot(iota((levels, half), 0) == iota((levels, half), 1), F32)
    own = lev_n * lev
    li, si = iota((levels, td), 0), iota((levels, td), 1)
    pick_div = onehot((li == own + si) & (si < lev_n), F32)
    pick_heat = onehot((li == own + si - lev_n) & (si >= lev_n) & (si < 2 * lev_n), F32)
    si, li = iota((td, levels), 0), iota((td, levels), 1)
    pick_div_t = onehot((li == own + si) & (si < lev_n), F32)
    pick_heat_t = onehot((li == own + si - lev_n) & (si >= lev_n) & (si < 2 * lev_n), F32)
    m_in = mi_ref[...]
    w1 = jnp.concatenate(
        [fdot(fdot(mode, m_in), pick_div), fdot(fdot(mode, fdot(m_in, g_ref[...])), pick_heat)], axis=0
    )
    w2 = fdot(fdot(pick_div_t, mo_ref[...]), mode_t) - 2.0 * fdot(fdot(pick_heat_t, mh_ref[...]), mode_t)
    rates = jnp.sum(
        jnp.where(iota((half, levels), 0) == iota((half, levels), 1), rates_ref[...][None, :], 0.0),
        axis=1, keepdims=True,
    )
    si = iota((td, 1), 0)
    stays = onehot(si >= lev_n, F32)

    def old_rows(p):
        slots = [s for g in groups[ends[p] : ends[p + 1]] for s in g]
        rows = (ends[p + 1] - ends[p]) * K
        total = None
        for c in range(2):
            if not any(s[2] == c for s in slots):
                continue
            row, col = iota((rows, 3 * lev_n), 0), iota((rows, 3 * lev_n), 1)
            src = jnp.full(row.shape, -1, jnp.int32)
            start = 0
            while start < len(slots):
                f, l, cc = slots[start]
                stop = start
                while stop < len(slots) and slots[stop] == (f, l + stop - start, cc):
                    stop += 1
                if cc == c:
                    src = jnp.where((row >= start) & (row < stop), row - start + f * lev_n + l, src)
                start = stop
            part = dot(onehot(col == src), old_all[:, c * nr : (c + 1) * nr])
            total = part if total is None else total + part
        return total

    old_all = jnp.concatenate([old_ref[f, 0] for f in range(3)], axis=0)
    olds = [old_rows(p) for p in range(3)]
    loads[12].wait()

    def turn(i, carry):
        at = pl.ds(pl.multiple_of(i * 128, 128), 128)
        turned[:, at] = leg[at, :].T
        return carry

    lax.fori_loop(0, nr // 128, turn, 0)

    def forward(p):
        g_n = ends[p + 1] - ends[p]
        cols = jnp.concatenate(
            [
                jnp.concatenate([recv1[d, :, base[g] : base[g] + jl] for d in range(n)], axis=1) * keep_b
                for g in range(ends[p], ends[p + 1])
            ],
            axis=0,
        )
        both = dot(cols, turned[...]).reshape(g_n, 2, K, nr)
        total = jnp.where(iota((g_n, K, nr), 2) < first_pad, both[:, 0], both[:, 1]).reshape(g_n * K, nr)
        return jnp.where(used, olds[p] + total, 0.0)

    def inverse(p, new):
        g_n = ends[p + 1] - ends[p]
        sides = jnp.stack(
            [
                jnp.where(first, new, 0.0).reshape(g_n, K, nr),
                jnp.where(first, 0.0, new).reshape(g_n, K, nr),
            ],
            axis=1,
        ).reshape(g_n * 16, nr).astype(BF16)
        out = dot(sides, leg[...])
        return [(out[i * 16 : (i + 1) * 16] * keep).astype(BF16) for i in range(g_n)]

    def exchange(p):
        return pltpu.make_async_remote_copy(
            src_ref=es.at[p], dst_ref=er.at[p], send_sem=es_sem.at[p], recv_sem=er_sem.at[p],
            device_id=(me, other), device_id_type=MESH,
        )

    grids = []

    def fill_piece(p):
        lo, hi = down[p], down[p + 1]
        for d in range(n if hi > lo else 0):
            row = [
                jnp.zeros((16, v), BF16) if g is None else grids[g][:, d * jl + u : d * jl + v]
                for g, u, v in lane_parts(base, jl, lo, hi)
            ]
            send2[d, :, lo:hi] = jnp.concatenate(row, axis=1) if len(row) > 1 else row[0]

    def send_piece(p):
        if down[p + 1] > down[p]:
            start_all(copy2, p, upwards)

    def arrive(p):
        if up[p + 1] > up[p]:
            whole(send1, recv1, up, s1, r1, p).wait_recv()

    def project(p, total):
        w1s, ts = split3(w1, total)
        res = dot(w1s, ts)
        proj = res[:half] + 2.0 * lam * res[half:]
        es[p - 1] = proj.astype(BF16)
        exchange(p - 1).start()
        return proj

    def step(p, total, proj):
        exchange(p - 1).wait()
        modal = (proj + er[p - 1].astype(F32)) / (1.0 + 4.0 * lam * rates)
        w2s, ms = split3(w2, modal)
        return jnp.where(used, total * stays + dot(w2s, ms), 0.0)

    arrive(0)
    vort = forward(0)
    grids += inverse(0, vort)
    fill_piece(0)
    arrive(1)
    total1 = forward(1)
    proj1 = project(1, total1)
    send_piece(0)
    arrive(2)
    total2 = forward(2)
    proj2 = project(2, total2)
    new1 = step(1, total1, proj1)
    grids += inverse(1, new1)
    fill_piece(1)
    send_piece(1)
    new2 = step(2, total2, proj2)
    grids += inverse(2, new2)
    fill_piece(2)
    send_piece(2)
    news = [vort, new1, new2]

    flat = [s for g in groups for s in g + [None] * (K - len(g))]
    starts = [e * K for e in ends]

    def row_of(slot):
        i = flat.index(slot)
        p = max(j for j in range(3) if starts[j] <= i)
        return p, i - starts[p]

    for c in range(2):
        for f in range(3):
            parts, l = [], 0
            while l < lev_n:
                p, i = row_of((f, l, c))
                stop = l
                while stop < lev_n and row_of((f, stop, c)) == (p, i + stop - l):
                    stop += 1
                parts.append(news[p][i : i + stop - l])
                l = stop
            rows = jnp.concatenate(parts, axis=0) if len(parts) > 1 else parts[0]
            spec_ref[f, 0, :, c * nr : (c + 1) * nr] = rows.astype(BF16)
    qr, qc = iota((4 * CHUNK * K, 1), 0), iota((1, CHUNK * 16), 1)
    q = qr % (4 * CHUNK)
    home = q // 4 * 16 + q // 2 % 2 * 8 + qr // (4 * CHUNK)
    backs = [onehot(qc == jnp.where(q % 2 == c, home, -1)) for c in range(2)]
    where = {s: (g, k) for g, slots in enumerate(groups) for k, s in enumerate(slots)}
    paired, single = [], []
    for g, slots in enumerate(groups):
        if all(c == 0 for f, l, c in slots):
            b = where[slots[0][0], slots[0][1], 1][0]
            if all(where[f, l, 1] == (b, k) for k, (f, l, c) in enumerate(slots)):
                paired.append((g, b))
    covered = {g for pair in paired for g in pair}
    for g, slots in enumerate(groups):
        if g not in covered:
            zero = [(f, l) for f, l, c in slots if c == 0]
            count = len(zero)
            sr = iota((4 * CHUNK * count, 1), 0)
            sq = sr % (4 * CHUNK)
            single.append(
                (g, zero, onehot(qc == sq // 4 * 16 + sq // 2 % 2 * 8 + sr // (4 * CHUNK) + count * (sq % 2)))
            )

    def stage(g):
        return min(p for p in range(3) if base[g] + jl <= down[p + 1])

    def wide(p, h, run):
        rows = recv2[h * CHUNK : (h + 1) * CHUNK, :, : down[p + 1]].reshape(CHUNK * 16, down[p + 1])
        rows = [rows[:, base[g] : base[g] + jl] for g in run]
        return jnp.concatenate(rows, axis=1) if len(rows) > 1 else rows[0]

    tops = {}
    for p in range(3):
        lo, hi = down[p], down[p + 1]
        if hi > lo:
            recv2[me, :, lo:hi] = send2[me, :, lo:hi]
            whole(send2, recv2, down, s2, r2, p).wait_recv()
        now = [(g, b) for g, b in paired if max(stage(g), stage(b)) == p]
        half_now = [g for g, b in paired if stage(g) == p]
        for h in range(n // CHUNK):
            qs = slice(h * 4 * CHUNK, (h + 1) * 4 * CHUNK)
            if half_now:
                got = dot(backs[0], wide(p, h, half_now))
                tops.update({(h, g): got[:, i * jl : (i + 1) * jl] for i, g in enumerate(half_now)})
            if now:
                got = dot(backs[1], wide(p, h, [b for g, b in now]))
                for i, (g, b) in enumerate(now):
                    piece = (got[:, i * jl : (i + 1) * jl] + tops[h, g]).astype(BF16)
                    for k, (f, l, c) in enumerate(groups[g]):
                        out_ref[f, l, qs] = piece[k * 4 * CHUNK : (k + 1) * 4 * CHUNK]
            for g, zero, perm in single:
                if stage(g) == p:
                    piece = dot(perm, wide(p, h, [g])).astype(BF16)
                    for k, (f, l) in enumerate(zero):
                        out_ref[f, l, qs] = piece[k * 4 * CHUNK : (k + 1) * 4 * CHUNK]

    for p in range(3):
        if up[p + 1] > up[p]:
            whole(send1, recv1, up, s1, r1, p).wait_send()
        if down[p + 1] > down[p]:
            whole(send2, recv2, down, s2, r2, p).wait_send()


def finish(spec, out, spec_hbm, out_hbm, sem):
    copies = [
        pltpu.make_async_copy(out, out_hbm, sem.at[0]),
        pltpu.make_async_copy(spec, spec_hbm, sem.at[1]),
    ]
    for copy in copies:
        copy.start()
    for copy in copies:
        copy.wait()


def body(
    fourier_in, spectral_old, legendre, g_matrix, modes_in, modes_out, mode_heating, mode_rates, pair_ids, lat_ids,
    limits,
):
    n, nlev = lax.axis_size("wave"), lax.axis_size("lev")
    fields, lev_n, jl, q_n = fourier_in.shape
    groups, ends, lanes, base, up, down = make_pieces(lev_n, jl)
    nr, nlat = legendre.shape[1:]
    half = (nlev * lev_n + 15) // 16 * 16
    hbm = pl.BlockSpec(memory_space=pltpu.HBM)
    vmem = pl.BlockSpec(memory_space=pltpu.VMEM)
    spec, out = pl.pallas_call(
        functools.partial(kernel, n, nlev),
        out_shape=(
            jax.ShapeDtypeStruct((fields, 1, lev_n, 2 * nr), BF16),
            jax.ShapeDtypeStruct((fields, lev_n, q_n, jl), BF16),
        ),
        in_specs=[hbm] * 11,
        out_specs=(vmem, vmem),
        scratch_shapes=[
            pltpu.VMEM((fields, lev_n, q_n, jl), BF16),
            pltpu.VMEM((fields, 1, lev_n, 2 * nr), BF16),
            pltpu.VMEM((nr, nlat), BF16),
            pltpu.VMEM(g_matrix.shape, F32),
            pltpu.VMEM(g_matrix.shape, F32),
            pltpu.VMEM(g_matrix.shape, F32),
            pltpu.VMEM(g_matrix.shape, F32),
            pltpu.VMEM(mode_rates.shape, F32),
            pltpu.SMEM(pair_ids.shape, jnp.int32),
            pltpu.VMEM(lat_ids.shape, jnp.int32),
            pltpu.VMEM(limits.shape, jnp.int32),
            pltpu.VMEM((n, 16, lanes), BF16),
            pltpu.VMEM((n, 16, lanes), BF16),
            pltpu.VMEM((n, 16, lanes), BF16),
            pltpu.VMEM((n, 16, lanes), BF16),
            pltpu.VMEM((2, half, nr), BF16),
            pltpu.VMEM((2, half, nr), BF16),
            pltpu.VMEM((nlat, nlat), BF16),
            pltpu.VMEM((nlat, nr), BF16),
            pltpu.SemaphoreType.DMA((13,)),
            pltpu.SemaphoreType.DMA((3,)),
            pltpu.SemaphoreType.DMA((3,)),
            pltpu.SemaphoreType.DMA((3,)),
            pltpu.SemaphoreType.DMA((3,)),
            pltpu.SemaphoreType.DMA((2,)),
            pltpu.SemaphoreType.DMA((2,)),
        ],
        compiler_params=pltpu.CompilerParams(
            collective_id=0, has_side_effects=True, vmem_limit_bytes=48 * 1024 * 1024
        ),
        cost_estimate=pl.CostEstimate(flops=10**9, bytes_accessed=8 * 10**6, transcendentals=0),
    )(
        *[
            pltpu.with_memory_space_constraint(x, pltpu.HBM)
            for x in (
                jnp.transpose(fourier_in, (0, 1, 3, 2)),
                jnp.transpose(spectral_old, (0, 2, 1, 3)),
                legendre,
                g_matrix,
                modes_in,
                modes_out,
                mode_heating,
                mode_rates,
                pair_ids,
                lat_ids,
                limits,
            )
        ]
    )
    spec, out = pl.pallas_call(
        finish,
        out_shape=(
            jax.ShapeDtypeStruct(spec.shape, BF16),
            jax.ShapeDtypeStruct(out.shape, BF16),
        ),
        in_specs=[vmem] * 2,
        out_specs=(hbm, hbm),
        scratch_shapes=[pltpu.SemaphoreType.DMA((2,))],
        compiler_params=pltpu.CompilerParams(vmem_limit_bytes=48 * 1024 * 1024),
        cost_estimate=pl.CostEstimate(flops=0, bytes_accessed=2 * 10**6, transcendentals=0),
    )(spec, out)
    return jnp.transpose(spec, (0, 2, 1, 3)), jnp.transpose(out, (0, 1, 3, 2))


def solution(mesh):
    wave = P(None, "lev", "wave", None)
    return jax.shard_map(
        body,
        mesh=mesh,
        in_specs=(wave, wave, P("wave", None, None)) + (P(),) * 8,
        out_specs=(wave, wave),
        check_vma=False,
    )
```

```python
import functools

import jax
import jax.numpy as jnp
from jax import lax
from jax.experimental import pallas as pl
from jax.experimental.pallas import tpu as pltpu
from jax.sharding import PartitionSpec as P

MMAX = 1280
BLOCK = 64
K = 8
CHUNK = 16
F32, BF16 = jnp.float32, jnp.bfloat16
MESH = pl.DeviceIdType.MESH
HI = lax.Precision.HIGHEST
NT = (((1,), (1,)), ((), ()))


def iota(shape, dim):
    return lax.broadcasted_iota(jnp.int32, shape, dim)


def dot(a, b):
    return jnp.dot(a, b, preferred_element_type=F32)


def fdot(a, b):
    return jnp.dot(a, b, precision=HI, preferred_element_type=F32)


def onehot(mask, dtype=BF16):
    return jnp.where(mask, 1.0, 0.0).astype(dtype)


def split3(left, right):
    lh = left.astype(BF16)
    ll = (left - lh.astype(F32)).astype(BF16)
    rh = right.astype(BF16)
    rl = (right - rh.astype(F32)).astype(BF16)
    return jnp.concatenate([lh, lh, ll], axis=1), jnp.concatenate([rh, rl, rh], axis=0)


def make_slots(lev_n):
    fill = -2 * lev_n % K
    rest = list(range(fill, lev_n))
    whole = len(rest) // K * K
    slots = []
    for levels in (rest[:whole], rest[whole:]):
        for c in range(2):
            slots += [(0, l, c) for l in levels]
    groups = [slots[i : i + K] for i in range(0, len(slots), K)]
    ends = [0, len(groups)]
    for c in range(2):
        slots = [(f, l, c) for f in (1, 2) for l in range(lev_n)] + [(0, l, c) for l in range(fill)]
        groups += [slots[i : i + K] for i in range(0, len(slots), K)]
        ends.append(len(groups))
    return groups, ends


def make_pieces(lev_n, jl):
    groups, ends = make_slots(lev_n)
    count = len(groups)
    lanes = (count * jl + 127) // 128 * 128
    pad = -ends[1] * jl % 128
    if count * jl + pad > lanes:
        pad = 0
    first = [g * jl + (pad if g >= ends[1] else 0) for g in range(count)] + [lanes]
    stops = [first[ends[1]], first[ends[2]], lanes]
    up = [min((e + 127) // 128 * 128, lanes) for e in stops]
    down = [e // 128 * 128 for e in stops]
    return groups, ends, lanes, first, [0] + up, [0] + down


def lane_parts(first, jl, lo, hi):
    parts, at = [], lo
    while at < hi:
        g = max(i for i in range(len(first) - 1) if first[i] <= at)
        if at < first[g] + jl:
            stop = min(hi, first[g] + jl)
            parts.append((g, at - first[g], stop - first[g]))
        else:
            stop = min(hi, first[g + 1])
            parts.append((None, 0, stop - at))
        at = stop
    return parts


def kernel(
    n, nlev, x_hbm, old_hbm, leg_hbm, g_hbm, mi_hbm, mo_hbm, mh_hbm, rates_hbm, pid_hbm, lat_hbm, lim_hbm,
    spec_ref, out_ref,
    x_ref, old_ref, leg, g_ref, mi_ref, mo_ref, mh_ref, rates_ref, pid_ref, lat_ref, lim_ref,
    send1, recv1, send2, recv2, es, er, hot, turned,
    in_sem, s1, r1, s2, r2, es_sem, er_sem,
):
    lev_n = x_ref.shape[1]
    jl = x_ref.shape[3]
    groups, ends, lanes, base, up, down = make_pieces(lev_n, jl)
    nr, nlat = leg_hbm.shape[1:]
    me, lev = lax.axis_index("wave"), lax.axis_index("lev")
    other = lax.rem(lev + 1, nlev)

    pairs = [(x_hbm.at[f], x_ref.at[f]) for f in (0, 1, 2)] + [
        (pid_hbm, pid_ref), (lat_hbm, lat_ref), (lim_hbm, lim_ref), (g_hbm, g_ref), (mi_hbm, mi_ref),
        (mo_hbm, mo_ref), (mh_hbm, mh_ref), (rates_hbm, rates_ref), (old_hbm, old_ref), (leg_hbm.at[0], leg),
    ]
    loads = [pltpu.make_async_copy(src, dst, in_sem.at[i]) for i, (src, dst) in enumerate(pairs)]
    for load in loads[:3]:
        load.start()
    def away(i):
        return lax.bitwise_xor(me, jnp.where(i % 2 == 0, n - 1 - i // 2, 1 + i // 2))

    def upwards(i):
        return jnp.where(i < me, i, i + 1)

    barrier = pltpu.get_barrier_semaphore()

    def greet(i, carry):
        pl.semaphore_signal(barrier, inc=1, device_id=(upwards(i), lev), device_id_type=MESH)
        return carry

    lax.fori_loop(0, n - 1, greet, 0)
    pl.semaphore_signal(barrier, inc=1, device_id=(me, other), device_id_type=MESH)
    for load in loads[3:]:
        load.start()

    pr, pc = iota((CHUNK * 16, 1), 0), iota((1, 4 * CHUNK * K), 1)
    home = pr % K * (4 * CHUNK) + pr // 16 * 4 + pr // 8 % 2 * 2

    def perm_of(g):
        part = jnp.zeros(pr.shape, jnp.int32)
        for k, (f, l, c) in enumerate(groups[g]):
            if c:
                part = jnp.where(pr % K == k, 1, part)
        return onehot(pc == home + part)

    def parts_of(g):
        return tuple(c for f, l, c in groups[g])

    perms = {}
    for g in range(len(groups)):
        if parts_of(g) not in perms:
            perms[parts_of(g)] = perm_of(g)

    def packed(g, h):
        blocks = [x_ref[f, l, h * 4 * CHUNK : (h + 1) * 4 * CHUNK] for f, l, c in groups[g]]
        blocks += [jnp.zeros_like(blocks[0])] * (K - len(blocks))
        return jnp.concatenate(blocks, axis=0)

    def pack_run(first, last, h):
        out, g = [], first
        while g < last:
            run = [g]
            while run[-1] + 1 < last and parts_of(run[-1] + 1) == parts_of(g):
                run.append(run[-1] + 1)
            data = [packed(i, h) for i in run]
            data = jnp.concatenate(data, axis=1) if len(run) > 1 else data[0]
            data = dot(perms[parts_of(g)], data).astype(BF16)
            out += [data[:, i * jl : (i + 1) * jl] for i in range(len(run))]
            g = run[-1] + 1
        return out

    def copy1(p, to):
        at = pl.ds(up[p], up[p + 1] - up[p])
        return pltpu.make_async_remote_copy(
            src_ref=send1.at[to, :, at], dst_ref=recv1.at[me, :, at], send_sem=s1.at[p], recv_sem=r1.at[p],
            device_id=(to, lev), device_id_type=MESH,
        )

    def copy2(p, to):
        at = pl.ds(down[p], down[p + 1] - down[p])
        return pltpu.make_async_remote_copy(
            src_ref=send2.at[to, :, at], dst_ref=recv2.at[me, :, at], send_sem=s2.at[p], recv_sem=r2.at[p],
            device_id=(to, lev), device_id_type=MESH,
        )

    def start_all(copy, p, order):
        def start(i, carry):
            copy(p, order(i)).start()
            return carry

        lax.fori_loop(0, n - 1, start, 0)

    def whole(src, dst, bounds, ss, rr, p):
        at = pl.ds(bounds[p], bounds[p + 1] - bounds[p])
        return pltpu.make_async_remote_copy(
            src_ref=src.at[pl.ds(0, n - 1), :, at], dst_ref=dst.at[pl.ds(0, n - 1), :, at], send_sem=ss.at[p],
            recv_sem=rr.at[p], device_id=(me, other), device_id_type=MESH,
        )

    done = 0
    held = {}
    for p in range(3):
        lo, hi = up[p], up[p + 1]
        if p == 0:
            loads[0].wait()
        if p == 1:
            loads[1].wait()
            loads[2].wait()
        if hi == lo:
            continue
        parts = lane_parts(base, jl, lo, hi)
        last = max([g + 1 for g, u, v in parts if g is not None] + [done])
        for h in range(n // CHUNK):
            held.update({(h, done + i): x for i, x in enumerate(pack_run(done, last, h))})
            row = [
                jnp.zeros((CHUNK * 16, v), BF16) if g is None else held[h, g][:, u:v] for g, u, v in parts
            ]
            row = jnp.concatenate(row, axis=1) if len(row) > 1 else row[0]
            send1[h * CHUNK : (h + 1) * CHUNK, :, lo:hi] = row.reshape(CHUNK, 16, hi - lo)
        done = last
        if p == 0:
            pl.semaphore_wait(barrier, n)
        start_all(copy1, p, away)
        recv1[me, :, lo:hi] = send1[me, :, lo:hi]

    for load in loads[3:12]:
        load.wait()

    hr = iota((16, nlat), 0)
    lim = lim_ref[...][None, :]
    lim_rows = jnp.where(hr == 0, lim // 8, jnp.where(hr == 1, lim % 8, 0)).astype(F32).astype(BF16)
    hot[...] = onehot(iota((nlat, nlat), 0) == lat_ref[...][None, :])
    got = dot(lim_rows, hot[...])
    row_limit = got[0:1] * 8.0 + got[1:2]
    a = pid_ref[me]
    wave = jnp.where(hr < 8, a, MMAX - 1 - a).astype(F32)
    keep = onehot(wave < row_limit, F32)
    keep_b = keep.astype(BF16)

    r = iota((1, nr), 1)
    first_pad = (MMAX - a + BLOCK - 1) // BLOCK * BLOCK
    first = r < first_pad
    used = (first & (r < MMAX - a)) | ((r >= first_pad) & (r - first_pad <= a))
    degree = jnp.where(first, a + r, MMAX - 1 - a + r - first_pad).astype(F32)
    lam = degree * (degree + 1.0) / float(MMAX * (MMAX - 1))

    levels = nlev * lev_n
    half = (levels + 15) // 16 * 16
    td = (ends[2] - ends[1]) * K
    mode = onehot(iota((half, levels), 0) == iota((half, levels), 1), F32)
    mode_t = onehot(iota((levels, half), 0) == iota((levels, half), 1), F32)
    own = lev_n * lev
    li, si = iota((levels, td), 0), iota((levels, td), 1)
    pick_div = onehot((li == own + si) & (si < lev_n), F32)
    pick_heat = onehot((li == own + si - lev_n) & (si >= lev_n) & (si < 2 * lev_n), F32)
    si, li = iota((td, levels), 0), iota((td, levels), 1)
    pick_div_t = onehot((li == own + si) & (si < lev_n), F32)
    pick_heat_t = onehot((li == own + si - lev_n) & (si >= lev_n) & (si < 2 * lev_n), F32)
    m_in = mi_ref[...]
    w1 = jnp.concatenate(
        [fdot(fdot(mode, m_in), pick_div), fdot(fdot(mode, fdot(m_in, g_ref[...])), pick_heat)], axis=0
    )
    w2 = fdot(fdot(pick_div_t, mo_ref[...]), mode_t) - 2.0 * fdot(fdot(pick_heat_t, mh_ref[...]), mode_t)
    rates = jnp.sum(
        jnp.where(iota((half, levels), 0) == iota((half, levels), 1), rates_ref[...][None, :], 0.0),
        axis=1, keepdims=True,
    )
    si = iota((td, 1), 0)
    stays = onehot(si >= lev_n, F32)

    def old_rows(p):
        slots = [s for g in groups[ends[p] : ends[p + 1]] for s in g]
        rows = (ends[p + 1] - ends[p]) * K
        total = None
        for c in range(2):
            if not any(s[2] == c for s in slots):
                continue
            row, col = iota((rows, 3 * lev_n), 0), iota((rows, 3 * lev_n), 1)
            src = jnp.full(row.shape, -1, jnp.int32)
            start = 0
            while start < len(slots):
                f, l, cc = slots[start]
                stop = start
                while stop < len(slots) and slots[stop] == (f, l + stop - start, cc):
                    stop += 1
                if cc == c:
                    src = jnp.where((row >= start) & (row < stop), row - start + f * lev_n + l, src)
                start = stop
            part = dot(onehot(col == src), old_all[:, c * nr : (c + 1) * nr])
            total = part if total is None else total + part
        return total

    old_all = jnp.concatenate([old_ref[f, 0] for f in range(3)], axis=0)
    olds = [old_rows(p) for p in range(3)]
    loads[12].wait()

    def turn(i, carry):
        at = pl.ds(pl.multiple_of(i * 128, 128), 128)
        turned[:, at] = leg[at, :].T
        return carry

    lax.fori_loop(0, nr // 128, turn, 0)

    def forward(p):
        g_n = ends[p + 1] - ends[p]
        cols = jnp.concatenate(
            [
                jnp.concatenate([recv1[d, :, base[g] : base[g] + jl] for d in range(n)], axis=1) * keep_b
                for g in range(ends[p], ends[p + 1])
            ],
            axis=0,
        )
        both = dot(cols, turned[...]).reshape(g_n, 2, K, nr)
        total = jnp.where(iota((g_n, K, nr), 2) < first_pad, both[:, 0], both[:, 1]).reshape(g_n * K, nr)
        return jnp.where(used, olds[p] + total, 0.0)

    def inverse(p, new):
        g_n = ends[p + 1] - ends[p]
        sides = jnp.stack(
            [
                jnp.where(first, new, 0.0).reshape(g_n, K, nr),
                jnp.where(first, 0.0, new).reshape(g_n, K, nr),
            ],
            axis=1,
        ).reshape(g_n * 16, nr).astype(BF16)
        out = dot(sides, leg[...])
        return [(out[i * 16 : (i + 1) * 16] * keep).astype(BF16) for i in range(g_n)]

    def exchange(p):
        return pltpu.make_async_remote_copy(
            src_ref=es.at[p], dst_ref=er.at[p], send_sem=es_sem.at[p], recv_sem=er_sem.at[p],
            device_id=(me, other), device_id_type=MESH,
        )

    grids = []

    def fill_piece(p):
        lo, hi = down[p], down[p + 1]
        for d in range(n if hi > lo else 0):
            row = [
                jnp.zeros((16, v), BF16) if g is None else grids[g][:, d * jl + u : d * jl + v]
                for g, u, v in lane_parts(base, jl, lo, hi)
            ]
            send2[d, :, lo:hi] = jnp.concatenate(row, axis=1) if len(row) > 1 else row[0]

    def send_piece(p):
        if down[p + 1] > down[p]:
            start_all(copy2, p, upwards)

    def arrive(p):
        if up[p + 1] > up[p]:
            whole(send1, recv1, up, s1, r1, p).wait_recv()

    def project(p, total):
        w1s, ts = split3(w1, total)
        res = dot(w1s, ts)
        proj = res[:half] + 2.0 * lam * res[half:]
        es[p - 1] = proj.astype(BF16)
        exchange(p - 1).start()
        return proj

    def step(p, total, proj):
        exchange(p - 1).wait()
        modal = (proj + er[p - 1].astype(F32)) / (1.0 + 4.0 * lam * rates)
        w2s, ms = split3(w2, modal)
        return jnp.where(used, total * stays + dot(w2s, ms), 0.0)

    arrive(0)
    vort = forward(0)
    grids += inverse(0, vort)
    fill_piece(0)
    arrive(1)
    total1 = forward(1)
    proj1 = project(1, total1)
    send_piece(0)
    arrive(2)
    total2 = forward(2)
    proj2 = project(2, total2)
    new1 = step(1, total1, proj1)
    grids += inverse(1, new1)
    fill_piece(1)
    send_piece(1)
    new2 = step(2, total2, proj2)
    grids += inverse(2, new2)
    fill_piece(2)
    send_piece(2)
    news = [vort, new1, new2]

    flat = [s for g in groups for s in g + [None] * (K - len(g))]
    starts = [e * K for e in ends]

    def row_of(slot):
        i = flat.index(slot)
        p = max(j for j in range(3) if starts[j] <= i)
        return p, i - starts[p]

    for c in range(2):
        for f in range(3):
            parts, l = [], 0
            while l < lev_n:
                p, i = row_of((f, l, c))
                stop = l
                while stop < lev_n and row_of((f, stop, c)) == (p, i + stop - l):
                    stop += 1
                parts.append(news[p][i : i + stop - l])
                l = stop
            rows = jnp.concatenate(parts, axis=0) if len(parts) > 1 else parts[0]
            spec_ref[f, 0, :, c * nr : (c + 1) * nr] = rows.astype(BF16)
    qr, qc = iota((4 * CHUNK * K, 1), 0), iota((1, CHUNK * 16), 1)
    q = qr % (4 * CHUNK)
    home = q // 4 * 16 + q // 2 % 2 * 8 + qr // (4 * CHUNK)
    backs = [onehot(qc == jnp.where(q % 2 == c, home, -1)) for c in range(2)]
    where = {s: (g, k) for g, slots in enumerate(groups) for k, s in enumerate(slots)}
    paired, single = [], []
    for g, slots in enumerate(groups):
        if all(c == 0 for f, l, c in slots):
            b = where[slots[0][0], slots[0][1], 1][0]
            if all(where[f, l, 1] == (b, k) for k, (f, l, c) in enumerate(slots)):
                paired.append((g, b))
    covered = {g for pair in paired for g in pair}
    for g, slots in enumerate(groups):
        if g not in covered:
            zero = [(f, l) for f, l, c in slots if c == 0]
            count = len(zero)
            sr = iota((4 * CHUNK * count, 1), 0)
            sq = sr % (4 * CHUNK)
            single.append(
                (g, zero, onehot(qc == sq // 4 * 16 + sq // 2 % 2 * 8 + sr // (4 * CHUNK) + count * (sq % 2)))
            )

    def stage(g):
        return min(p for p in range(3) if base[g] + jl <= down[p + 1])

    def wide(p, h, run):
        rows = recv2[h * CHUNK : (h + 1) * CHUNK, :, : down[p + 1]].reshape(CHUNK * 16, down[p + 1])
        rows = [rows[:, base[g] : base[g] + jl] for g in run]
        return jnp.concatenate(rows, axis=1) if len(rows) > 1 else rows[0]

    tops = {}
    for p in range(3):
        lo, hi = down[p], down[p + 1]
        if hi > lo:
            recv2[me, :, lo:hi] = send2[me, :, lo:hi]
            whole(send2, recv2, down, s2, r2, p).wait_recv()
        now = [(g, b) for g, b in paired if max(stage(g), stage(b)) == p]
        half_now = [g for g, b in paired if stage(g) == p]
        for h in range(n // CHUNK):
            qs = slice(h * 4 * CHUNK, (h + 1) * 4 * CHUNK)
            if half_now:
                got = dot(backs[0], wide(p, h, half_now))
                tops.update({(h, g): got[:, i * jl : (i + 1) * jl] for i, g in enumerate(half_now)})
            if now:
                got = dot(backs[1], wide(p, h, [b for g, b in now]))
                for i, (g, b) in enumerate(now):
                    piece = (got[:, i * jl : (i + 1) * jl] + tops[h, g]).astype(BF16)
                    for k, (f, l, c) in enumerate(groups[g]):
                        out_ref[f, l, qs] = piece[k * 4 * CHUNK : (k + 1) * 4 * CHUNK]
            for g, zero, perm in single:
                if stage(g) == p:
                    piece = dot(perm, wide(p, h, [g])).astype(BF16)
                    for k, (f, l) in enumerate(zero):
                        out_ref[f, l, qs] = piece[k * 4 * CHUNK : (k + 1) * 4 * CHUNK]

    for p in range(3):
        if up[p + 1] > up[p]:
            whole(send1, recv1, up, s1, r1, p).wait_send()
        if down[p + 1] > down[p]:
            whole(send2, recv2, down, s2, r2, p).wait_send()


def finish(spec, out, spec_hbm, out_hbm, sem):
    copies = [
        pltpu.make_async_copy(out, out_hbm, sem.at[0]),
        pltpu.make_async_copy(spec, spec_hbm, sem.at[1]),
    ]
    for copy in copies:
        copy.start()
    for copy in copies:
        copy.wait()


def body(
    fourier_in, spectral_old, legendre, g_matrix, modes_in, modes_out, mode_heating, mode_rates, pair_ids, lat_ids,
    limits,
):
    n, nlev = lax.axis_size("wave"), lax.axis_size("lev")
    fields, lev_n, jl, q_n = fourier_in.shape
    groups, ends, lanes, base, up, down = make_pieces(lev_n, jl)
    nr, nlat = legendre.shape[1:]
    half = (nlev * lev_n + 15) // 16 * 16
    hbm = pl.BlockSpec(memory_space=pltpu.HBM)
    vmem = pl.BlockSpec(memory_space=pltpu.VMEM)
    spec, out = pl.pallas_call(
        functools.partial(kernel, n, nlev),
        out_shape=(
            jax.ShapeDtypeStruct((fields, 1, lev_n, 2 * nr), BF16),
            jax.ShapeDtypeStruct((fields, lev_n, q_n, jl), BF16),
        ),
        in_specs=[hbm] * 11,
        out_specs=(vmem, vmem),
        scratch_shapes=[
            pltpu.VMEM((fields, lev_n, q_n, jl), BF16),
            pltpu.VMEM((fields, 1, lev_n, 2 * nr), BF16),
            pltpu.VMEM((nr, nlat), BF16),
            pltpu.VMEM(g_matrix.shape, F32),
            pltpu.VMEM(g_matrix.shape, F32),
            pltpu.VMEM(g_matrix.shape, F32),
            pltpu.VMEM(g_matrix.shape, F32),
            pltpu.VMEM(mode_rates.shape, F32),
            pltpu.SMEM(pair_ids.shape, jnp.int32),
            pltpu.VMEM(lat_ids.shape, jnp.int32),
            pltpu.VMEM(limits.shape, jnp.int32),
            pltpu.VMEM((n, 16, lanes), BF16),
            pltpu.VMEM((n, 16, lanes), BF16),
            pltpu.VMEM((n, 16, lanes), BF16),
            pltpu.VMEM((n, 16, lanes), BF16),
            pltpu.VMEM((2, half, nr), BF16),
            pltpu.VMEM((2, half, nr), BF16),
            pltpu.VMEM((nlat, nlat), BF16),
            pltpu.VMEM((nlat, nr), BF16),
            pltpu.SemaphoreType.DMA((13,)),
            pltpu.SemaphoreType.DMA((3,)),
            pltpu.SemaphoreType.DMA((3,)),
            pltpu.SemaphoreType.DMA((3,)),
            pltpu.SemaphoreType.DMA((3,)),
            pltpu.SemaphoreType.DMA((2,)),
            pltpu.SemaphoreType.DMA((2,)),
        ],
        compiler_params=pltpu.CompilerParams(
            collective_id=0, has_side_effects=True, vmem_limit_bytes=48 * 1024 * 1024
        ),
        cost_estimate=pl.CostEstimate(flops=10**9, bytes_accessed=8 * 10**6, transcendentals=0),
    )(
        *[
            pltpu.with_memory_space_constraint(x, pltpu.HBM)
            for x in (
                jnp.transpose(fourier_in, (0, 1, 3, 2)),
                jnp.transpose(spectral_old, (0, 2, 1, 3)),
                legendre,
                g_matrix,
                modes_in,
                modes_out,
                mode_heating,
                mode_rates,
                pair_ids,
                lat_ids,
                limits,
            )
        ]
    )
    spec, out = pl.pallas_call(
        finish,
        out_shape=(
            jax.ShapeDtypeStruct(spec.shape, BF16),
            jax.ShapeDtypeStruct(out.shape, BF16),
        ),
        in_specs=[vmem] * 2,
        out_specs=(hbm, hbm),
        scratch_shapes=[pltpu.SemaphoreType.DMA((2,))],
        compiler_params=pltpu.CompilerParams(vmem_limit_bytes=48 * 1024 * 1024),
        cost_estimate=pl.CostEstimate(flops=0, bytes_accessed=2 * 10**6, transcendentals=0),
    )(spec, out)
    return jnp.transpose(spec, (0, 2, 1, 3)), jnp.transpose(out, (0, 1, 3, 2))


def solution(mesh):
    wave = P(None, "lev", "wave", None)
    return jax.shard_map(
        body,
        mesh=mesh,
        in_specs=(wave, wave, P("wave", None, None)) + (P(),) * 8,
        out_specs=(wave, wave),
        check_vma=False,
    )
```

```python
import functools

import jax
import jax.numpy as jnp
from jax import lax
from jax.experimental import pallas as pl
from jax.experimental.pallas import tpu as pltpu
from jax.sharding import PartitionSpec as P

MMAX = 1280
BLOCK = 64
K = 8
CHUNK = 16
F32, BF16 = jnp.float32, jnp.bfloat16
MESH = pl.DeviceIdType.MESH
HI = lax.Precision.HIGHEST
NT = (((1,), (1,)), ((), ()))


def iota(shape, dim):
    return lax.broadcasted_iota(jnp.int32, shape, dim)


def dot(a, b):
    return jnp.dot(a, b, preferred_element_type=F32)


def fdot(a, b):
    return jnp.dot(a, b, precision=HI, preferred_element_type=F32)


def onehot(mask, dtype=BF16):
    return jnp.where(mask, 1.0, 0.0).astype(dtype)


def split3(left, right):
    lh = left.astype(BF16)
    ll = (left - lh.astype(F32)).astype(BF16)
    rh = right.astype(BF16)
    rl = (right - rh.astype(F32)).astype(BF16)
    return jnp.concatenate([lh, lh, ll], axis=1), jnp.concatenate([rh, rl, rh], axis=0)


def make_slots(lev_n):
    fill = -2 * lev_n % K
    rest = list(range(fill, lev_n))
    whole = len(rest) // K * K
    slots = []
    for levels in (rest[:whole], rest[whole:]):
        for c in range(2):
            slots += [(0, l, c) for l in levels]
    groups = [slots[i : i + K] for i in range(0, len(slots), K)]
    ends = [0, len(groups)]
    for c in range(2):
        slots = [(f, l, c) for f in (1, 2) for l in range(lev_n)] + [(0, l, c) for l in range(fill)]
        groups += [slots[i : i + K] for i in range(0, len(slots), K)]
        ends.append(len(groups))
    return groups, ends


def make_pieces(lev_n, jl):
    groups, ends = make_slots(lev_n)
    count = len(groups)
    lanes = (count * jl + 127) // 128 * 128
    pad = -ends[1] * jl % 128
    if count * jl + pad > lanes:
        pad = 0
    first = [g * jl + (pad if g >= ends[1] else 0) for g in range(count)] + [lanes]
    stops = [first[ends[1]], first[ends[2]], lanes]
    up = [min((e + 127) // 128 * 128, lanes) for e in stops]
    down = [e // 128 * 128 for e in stops]
    return groups, ends, lanes, first, [0] + up, [0] + down


def lane_parts(first, jl, lo, hi):
    parts, at = [], lo
    while at < hi:
        g = max(i for i in range(len(first) - 1) if first[i] <= at)
        if at < first[g] + jl:
            stop = min(hi, first[g] + jl)
            parts.append((g, at - first[g], stop - first[g]))
        else:
            stop = min(hi, first[g + 1])
            parts.append((None, 0, stop - at))
        at = stop
    return parts


def kernel(
    n, nlev, x_hbm, old_hbm, leg_hbm, g_hbm, mi_hbm, mo_hbm, mh_hbm, rates_hbm, pid_hbm, lat_hbm, lim_hbm,
    spec_ref, out_ref,
    x_ref, old_ref, leg, g_ref, mi_ref, mo_ref, mh_ref, rates_ref, pid_ref, lat_ref, lim_ref,
    send1, recv1, send2, recv2, es, er, hot, turned,
    in_sem, s1, r1, s2, r2, es_sem, er_sem,
):
    lev_n = x_ref.shape[1]
    jl = x_ref.shape[3]
    groups, ends, lanes, base, up, down = make_pieces(lev_n, jl)
    nr, nlat = leg_hbm.shape[1:]
    me, lev = lax.axis_index("wave"), lax.axis_index("lev")
    other = lax.rem(lev + 1, nlev)

    pairs = [(x_hbm.at[f], x_ref.at[f]) for f in (0, 1, 2)] + [
        (pid_hbm, pid_ref), (lat_hbm, lat_ref), (lim_hbm, lim_ref), (g_hbm, g_ref), (mi_hbm, mi_ref),
        (mo_hbm, mo_ref), (mh_hbm, mh_ref), (rates_hbm, rates_ref), (old_hbm, old_ref), (leg_hbm.at[0], leg),
    ]
    loads = [pltpu.make_async_copy(src, dst, in_sem.at[i]) for i, (src, dst) in enumerate(pairs)]
    for load in loads[:3]:
        load.start()
    plane = n // 4

    def away(i):
        return lax.bitwise_xor(me, jnp.where((lev == 0) & (i % 2 == 0), n - 1 - i // 2, jnp.where(lev == 0, 1 + i // 2, n - 1 - i)))

    def upwards(i):
        return jnp.where(i < me, i, i + 1)

    barrier = pltpu.get_barrier_semaphore()

    def greet(i, carry):
        pl.semaphore_signal(barrier, inc=1, device_id=(upwards(i), lev), device_id_type=MESH)
        return carry

    lax.fori_loop(0, n - 1, greet, 0)
    pl.semaphore_signal(barrier, inc=1, device_id=(me, other), device_id_type=MESH)
    for load in loads[3:]:
        load.start()

    pr, pc = iota((CHUNK * 16, 1), 0), iota((1, 4 * CHUNK * K), 1)
    home = pr % K * (4 * CHUNK) + pr // 16 * 4 + pr // 8 % 2 * 2

    def perm_of(g):
        part = jnp.zeros(pr.shape, jnp.int32)
        for k, (f, l, c) in enumerate(groups[g]):
            if c:
                part = jnp.where(pr % K == k, 1, part)
        return onehot(pc == home + part)

    def parts_of(g):
        return tuple(c for f, l, c in groups[g])

    perms = {}
    for g in range(len(groups)):
        if parts_of(g) not in perms:
            perms[parts_of(g)] = perm_of(g)

    def packed(g, h):
        blocks = [x_ref[f, l, h * 4 * CHUNK : (h + 1) * 4 * CHUNK] for f, l, c in groups[g]]
        blocks += [jnp.zeros_like(blocks[0])] * (K - len(blocks))
        return jnp.concatenate(blocks, axis=0)

    def pack_run(first, last, h):
        out, g = [], first
        while g < last:
            run = [g]
            while run[-1] + 1 < last and parts_of(run[-1] + 1) == parts_of(g):
                run.append(run[-1] + 1)
            data = [packed(i, h) for i in run]
            data = jnp.concatenate(data, axis=1) if len(run) > 1 else data[0]
            data = dot(perms[parts_of(g)], data).astype(BF16)
            out += [data[:, i * jl : (i + 1) * jl] for i in range(len(run))]
            g = run[-1] + 1
        return out

    def copy1(p, to):
        at = pl.ds(up[p], up[p + 1] - up[p])
        return pltpu.make_async_remote_copy(
            src_ref=send1.at[to, :, at], dst_ref=recv1.at[me, :, at], send_sem=s1.at[p], recv_sem=r1.at[p],
            device_id=(to, lev), device_id_type=MESH,
        )

    def copy2(p, to):
        at = pl.ds(down[p], down[p + 1] - down[p])
        return pltpu.make_async_remote_copy(
            src_ref=send2.at[to, :, at], dst_ref=recv2.at[me, :, at], send_sem=s2.at[p], recv_sem=r2.at[p + me // plane if p == 2 else p],
            device_id=(to, lev), device_id_type=MESH,
        )

    def start_all(copy, p, order):
        def start(i, carry):
            copy(p, order(i)).start()
            return carry

        lax.fori_loop(0, n - 1, start, 0)

    def whole(src, dst, bounds, ss, rr, p):
        at = pl.ds(bounds[p], bounds[p + 1] - bounds[p])
        return pltpu.make_async_remote_copy(
            src_ref=src.at[pl.ds(0, n - 1), :, at], dst_ref=dst.at[pl.ds(0, n - 1), :, at], send_sem=ss.at[p],
            recv_sem=rr.at[p], device_id=(me, other), device_id_type=MESH,
        )

    done = 0
    held = {}
    for p in range(3):
        lo, hi = up[p], up[p + 1]
        if p == 0:
            loads[0].wait()
        if p == 1:
            loads[1].wait()
            loads[2].wait()
        if hi == lo:
            continue
        parts = lane_parts(base, jl, lo, hi)
        last = max([g + 1 for g, u, v in parts if g is not None] + [done])
        for h in range(n // CHUNK):
            held.update({(h, done + i): x for i, x in enumerate(pack_run(done, last, h))})
            row = [
                jnp.zeros((CHUNK * 16, v), BF16) if g is None else held[h, g][:, u:v] for g, u, v in parts
            ]
            row = jnp.concatenate(row, axis=1) if len(row) > 1 else row[0]
            send1[h * CHUNK : (h + 1) * CHUNK, :, lo:hi] = row.reshape(CHUNK, 16, hi - lo)
        done = last
        if p == 0:
            pl.semaphore_wait(barrier, n)
        start_all(copy1, p, away)
        recv1[me, :, lo:hi] = send1[me, :, lo:hi]

    for load in loads[3:12]:
        load.wait()

    hr = iota((16, nlat), 0)
    lim = lim_ref[...][None, :]
    lim_rows = jnp.where(hr == 0, lim // 8, jnp.where(hr == 1, lim % 8, 0)).astype(F32).astype(BF16)
    hot[...] = onehot(iota((nlat, nlat), 0) == lat_ref[...][None, :])
    got = dot(lim_rows, hot[...])
    row_limit = got[0:1] * 8.0 + got[1:2]
    a = pid_ref[me]
    wave = jnp.where(hr < 8, a, MMAX - 1 - a).astype(F32)
    keep = onehot(wave < row_limit, F32)
    keep_b = keep.astype(BF16)

    r = iota((1, nr), 1)
    first_pad = (MMAX - a + BLOCK - 1) // BLOCK * BLOCK
    first = r < first_pad
    used = (first & (r < MMAX - a)) | ((r >= first_pad) & (r - first_pad <= a))
    degree = jnp.where(first, a + r, MMAX - 1 - a + r - first_pad).astype(F32)
    lam = degree * (degree + 1.0) / float(MMAX * (MMAX - 1))

    levels = nlev * lev_n
    half = (levels + 15) // 16 * 16
    td = (ends[2] - ends[1]) * K
    mode = onehot(iota((half, levels), 0) == iota((half, levels), 1), F32)
    mode_t = onehot(iota((levels, half), 0) == iota((levels, half), 1), F32)
    own = lev_n * lev
    li, si = iota((levels, td), 0), iota((levels, td), 1)
    pick_div = onehot((li == own + si) & (si < lev_n), F32)
    pick_heat = onehot((li == own + si - lev_n) & (si >= lev_n) & (si < 2 * lev_n), F32)
    si, li = iota((td, levels), 0), iota((td, levels), 1)
    pick_div_t = onehot((li == own + si) & (si < lev_n), F32)
    pick_heat_t = onehot((li == own + si - lev_n) & (si >= lev_n) & (si < 2 * lev_n), F32)
    m_in = mi_ref[...]
    w1 = jnp.concatenate(
        [fdot(fdot(mode, m_in), pick_div), fdot(fdot(mode, fdot(m_in, g_ref[...])), pick_heat)], axis=0
    )
    w2 = fdot(fdot(pick_div_t, mo_ref[...]), mode_t) - 2.0 * fdot(fdot(pick_heat_t, mh_ref[...]), mode_t)
    rates = jnp.sum(
        jnp.where(iota((half, levels), 0) == iota((half, levels), 1), rates_ref[...][None, :], 0.0),
        axis=1, keepdims=True,
    )
    si = iota((td, 1), 0)
    stays = onehot(si >= lev_n, F32)

    def old_rows(p):
        slots = [s for g in groups[ends[p] : ends[p + 1]] for s in g]
        rows = (ends[p + 1] - ends[p]) * K
        total = None
        for c in range(2):
            if not any(s[2] == c for s in slots):
                continue
            row, col = iota((rows, 3 * lev_n), 0), iota((rows, 3 * lev_n), 1)
            src = jnp.full(row.shape, -1, jnp.int32)
            start = 0
            while start < len(slots):
                f, l, cc = slots[start]
                stop = start
                while stop < len(slots) and slots[stop] == (f, l + stop - start, cc):
                    stop += 1
                if cc == c:
                    src = jnp.where((row >= start) & (row < stop), row - start + f * lev_n + l, src)
                start = stop
            part = dot(onehot(col == src), old_all[:, c * nr : (c + 1) * nr])
            total = part if total is None else total + part
        return total

    old_all = jnp.concatenate([old_ref[f, 0] for f in range(3)], axis=0)
    olds = [old_rows(p) for p in range(3)]
    loads[12].wait()

    def turn(i, carry):
        at = pl.ds(pl.multiple_of(i * 128, 128), 128)
        turned[:, at] = leg[at, :].T
        return carry

    lax.fori_loop(0, nr // 128, turn, 0)

    def forward(p):
        g_n = ends[p + 1] - ends[p]
        cols = jnp.concatenate(
            [
                jnp.concatenate([recv1[d, :, base[g] : base[g] + jl] for d in range(n)], axis=1) * keep_b
                for g in range(ends[p], ends[p + 1])
            ],
            axis=0,
        )
        both = dot(cols, turned[...]).reshape(g_n, 2, K, nr)
        total = jnp.where(iota((g_n, K, nr), 2) < first_pad, both[:, 0], both[:, 1]).reshape(g_n * K, nr)
        return jnp.where(used, olds[p] + total, 0.0)

    def inverse(p, new):
        g_n = ends[p + 1] - ends[p]
        sides = jnp.stack(
            [
                jnp.where(first, new, 0.0).reshape(g_n, K, nr),
                jnp.where(first, 0.0, new).reshape(g_n, K, nr),
            ],
            axis=1,
        ).reshape(g_n * 16, nr).astype(BF16)
        out = dot(sides, leg[...])
        return [(out[i * 16 : (i + 1) * 16] * keep).astype(BF16) for i in range(g_n)]

    def exchange(p):
        return pltpu.make_async_remote_copy(
            src_ref=es.at[p], dst_ref=er.at[p], send_sem=es_sem.at[p], recv_sem=er_sem.at[p],
            device_id=(me, other), device_id_type=MESH,
        )

    grids = []

    def fill_piece(p):
        lo, hi = down[p], down[p + 1]
        for d in range(n if hi > lo else 0):
            row = [
                jnp.zeros((16, v), BF16) if g is None else grids[g][:, d * jl + u : d * jl + v]
                for g, u, v in lane_parts(base, jl, lo, hi)
            ]
            send2[d, :, lo:hi] = jnp.concatenate(row, axis=1) if len(row) > 1 else row[0]

    def send_piece(p):
        if down[p + 1] > down[p]:
            start_all(copy2, p, upwards if p else away)

    def arrive(p):
        if up[p + 1] > up[p]:
            whole(send1, recv1, up, s1, r1, p).wait_recv()

    def project(p, total):
        w1s, ts = split3(w1, total)
        res = dot(w1s, ts)
        proj = res[:half] + 2.0 * lam * res[half:]
        es[p - 1] = proj.astype(BF16)
        exchange(p - 1).start()
        return proj

    def step(p, total, proj):
        exchange(p - 1).wait()
        modal = (proj + er[p - 1].astype(F32)) / (1.0 + 4.0 * lam * rates)
        w2s, ms = split3(w2, modal)
        return jnp.where(used, total * stays + dot(w2s, ms), 0.0)

    arrive(0)
    vort = forward(0)
    grids += inverse(0, vort)
    fill_piece(0)
    arrive(1)
    total1 = forward(1)
    proj1 = project(1, total1)
    send_piece(0)
    arrive(2)
    total2 = forward(2)
    proj2 = project(2, total2)
    new1 = step(1, total1, proj1)
    grids += inverse(1, new1)
    fill_piece(1)
    send_piece(1)
    new2 = step(2, total2, proj2)
    grids += inverse(2, new2)
    fill_piece(2)
    send_piece(2)
    news = [vort, new1, new2]

    flat = [s for g in groups for s in g + [None] * (K - len(g))]
    starts = [e * K for e in ends]

    def row_of(slot):
        i = flat.index(slot)
        p = max(j for j in range(3) if starts[j] <= i)
        return p, i - starts[p]

    for c in range(2):
        for f in range(3):
            parts, l = [], 0
            while l < lev_n:
                p, i = row_of((f, l, c))
                stop = l
                while stop < lev_n and row_of((f, stop, c)) == (p, i + stop - l):
                    stop += 1
                parts.append(news[p][i : i + stop - l])
                l = stop
            rows = jnp.concatenate(parts, axis=0) if len(parts) > 1 else parts[0]
            spec_ref[f, 0, :, c * nr : (c + 1) * nr] = rows.astype(BF16)
    qr, qc = iota((4 * CHUNK * K, 1), 0), iota((1, CHUNK * 16), 1)
    q = qr % (4 * CHUNK)
    home = q // 4 * 16 + q // 2 % 2 * 8 + qr // (4 * CHUNK)
    backs = [onehot(qc == jnp.where(q % 2 == c, home, -1)) for c in range(2)]
    where = {s: (g, k) for g, slots in enumerate(groups) for k, s in enumerate(slots)}
    paired, single = [], []
    for g, slots in enumerate(groups):
        if all(c == 0 for f, l, c in slots):
            b = where[slots[0][0], slots[0][1], 1][0]
            if all(where[f, l, 1] == (b, k) for k, (f, l, c) in enumerate(slots)):
                paired.append((g, b))
    covered = {g for pair in paired for g in pair}
    for g, slots in enumerate(groups):
        if g not in covered:
            zero = [(f, l) for f, l, c in slots if c == 0]
            count = len(zero)
            sr = iota((4 * CHUNK * count, 1), 0)
            sq = sr % (4 * CHUNK)
            single.append(
                (g, zero, onehot(qc == sq // 4 * 16 + sq // 2 % 2 * 8 + sr // (4 * CHUNK) + count * (sq % 2)))
            )

    def stage(g):
        return min(p for p in range(3) if base[g] + jl <= down[p + 1])

    def wide(p, h, run):
        rows = recv2[h * CHUNK : (h + 1) * CHUNK, :, : down[p + 1]].reshape(CHUNK * 16, down[p + 1])
        rows = [rows[:, base[g] : base[g] + jl] for g in run]
        return jnp.concatenate(rows, axis=1) if len(rows) > 1 else rows[0]

    for p in range(2):
        lo, hi = down[p], down[p + 1]
        if hi > lo:
            recv2[me, :, lo:hi] = send2[me, :, lo:hi]
            whole(send2, recv2, down, s2, r2, p).wait_recv()
        now = [(g, b) for g, b in paired if max(stage(g), stage(b)) == p]
        for h in range(n // CHUNK):
            qs = slice(h * 4 * CHUNK, (h + 1) * 4 * CHUNK)
            if now:
                got = dot(backs[0], wide(p, h, [g for g, b in now])) + dot(backs[1], wide(p, h, [b for g, b in now]))
                for i, (g, b) in enumerate(now):
                    piece = got[:, i * jl : (i + 1) * jl].astype(BF16)
                    for k, (f, l, c) in enumerate(groups[g]):
                        out_ref[f, l, qs] = piece[k * 4 * CHUNK : (k + 1) * 4 * CHUNK]
            for g, zero, perm in single:
                if stage(g) == p:
                    piece = dot(perm, wide(p, h, [g])).astype(BF16)
                    for k, (f, l) in enumerate(zero):
                        out_ref[f, l, qs] = piece[k * 4 * CHUNK : (k + 1) * 4 * CHUNK]

    for p in range(3):
        if up[p + 1] > up[p]:
            whole(send1, recv1, up, s1, r1, p).wait_send()
        if down[p + 1] > down[p]:
            whole(send2, recv2, down, s2, r2, p).wait_send()

    lo, hi = down[2], down[3]
    recv2[me, :, lo:hi] = send2[me, :, lo:hi]
    now = [(g, b) for g, b in paired if max(stage(g), stage(b)) == 2]
    wide_q = 4 * plane
    qr, qc = iota((wide_q * K, 1), 0), iota((1, 2 * plane * 16), 1)
    q = qr % wide_q
    turn_back = onehot(qc == q % 2 * (plane * 16) + q // 4 * 16 + q // 2 % 2 * 8 + qr // wide_q)
    for i in range(4):
        t = lax.bitwise_xor(me // plane, i)
        count = plane if i else plane - 1
        landed = recv2.at[pl.ds(0, count), :, pl.ds(lo, hi - lo)]
        pltpu.make_async_remote_copy(
            src_ref=send2.at[pl.ds(0, count), :, pl.ds(lo, hi - lo)], dst_ref=landed, send_sem=s2.at[2],
            recv_sem=r2.at[2 + t], device_id=(me, other), device_id_type=MESH,
        ).wait_recv()
        rows = recv2[pl.ds(t * plane, plane)].reshape(plane * 16, lanes)
        data = [
            jnp.concatenate([rows[:, base[g] : base[g] + jl] for g in run], axis=1) for run in zip(*now)
        ]
        got = dot(turn_back, jnp.concatenate(data, axis=0)).astype(BF16)
        at = pl.ds(pl.multiple_of(t * wide_q, wide_q), wide_q)
        for m, (g, b) in enumerate(now):
            for k, (f, l, c) in enumerate(groups[g]):
                out_ref[f, l, at] = got[k * wide_q : (k + 1) * wide_q, m * jl : (m + 1) * jl]


def finish(spec, out, spec_hbm, out_hbm, sem):
    copies = [
        pltpu.make_async_copy(out, out_hbm, sem.at[0]),
        pltpu.make_async_copy(spec, spec_hbm, sem.at[1]),
    ]
    for copy in copies:
        copy.start()
    for copy in copies:
        copy.wait()


def body(
    fourier_in, spectral_old, legendre, g_matrix, modes_in, modes_out, mode_heating, mode_rates, pair_ids, lat_ids,
    limits,
):
    n, nlev = lax.axis_size("wave"), lax.axis_size("lev")
    fields, lev_n, jl, q_n = fourier_in.shape
    groups, ends, lanes, base, up, down = make_pieces(lev_n, jl)
    nr, nlat = legendre.shape[1:]
    half = (nlev * lev_n + 15) // 16 * 16
    hbm = pl.BlockSpec(memory_space=pltpu.HBM)
    vmem = pl.BlockSpec(memory_space=pltpu.VMEM)
    spec, out = pl.pallas_call(
        functools.partial(kernel, n, nlev),
        out_shape=(
            jax.ShapeDtypeStruct((fields, 1, lev_n, 2 * nr), BF16),
            jax.ShapeDtypeStruct((fields, lev_n, q_n, jl), BF16),
        ),
        in_specs=[hbm] * 11,
        out_specs=(vmem, vmem),
        scratch_shapes=[
            pltpu.VMEM((fields, lev_n, q_n, jl), BF16),
            pltpu.VMEM((fields, 1, lev_n, 2 * nr), BF16),
            pltpu.VMEM((nr, nlat), BF16),
            pltpu.VMEM(g_matrix.shape, F32),
            pltpu.VMEM(g_matrix.shape, F32),
            pltpu.VMEM(g_matrix.shape, F32),
            pltpu.VMEM(g_matrix.shape, F32),
            pltpu.VMEM(mode_rates.shape, F32),
            pltpu.SMEM(pair_ids.shape, jnp.int32),
            pltpu.VMEM(lat_ids.shape, jnp.int32),
            pltpu.VMEM(limits.shape, jnp.int32),
            pltpu.VMEM((n, 16, lanes), BF16),
            pltpu.VMEM((n, 16, lanes), BF16),
            pltpu.VMEM((n, 16, lanes), BF16),
            pltpu.VMEM((n, 16, lanes), BF16),
            pltpu.VMEM((2, half, nr), BF16),
            pltpu.VMEM((2, half, nr), BF16),
            pltpu.VMEM((nlat, nlat), BF16),
            pltpu.VMEM((nlat, nr), BF16),
            pltpu.SemaphoreType.DMA((13,)),
            pltpu.SemaphoreType.DMA((3,)),
            pltpu.SemaphoreType.DMA((3,)),
            pltpu.SemaphoreType.DMA((3,)),
            pltpu.SemaphoreType.DMA((6,)),
            pltpu.SemaphoreType.DMA((2,)),
            pltpu.SemaphoreType.DMA((2,)),
        ],
        compiler_params=pltpu.CompilerParams(
            collective_id=0, has_side_effects=True, vmem_limit_bytes=48 * 1024 * 1024
        ),
        cost_estimate=pl.CostEstimate(flops=10**9, bytes_accessed=8 * 10**6, transcendentals=0),
    )(
        *[
            pltpu.with_memory_space_constraint(x, pltpu.HBM)
            for x in (
                jnp.transpose(fourier_in, (0, 1, 3, 2)),
                jnp.transpose(spectral_old, (0, 2, 1, 3)),
                legendre,
                g_matrix,
                modes_in,
                modes_out,
                mode_heating,
                mode_rates,
                pair_ids,
                lat_ids,
                limits,
            )
        ]
    )
    spec, out = pl.pallas_call(
        finish,
        out_shape=(
            jax.ShapeDtypeStruct(spec.shape, BF16),
            jax.ShapeDtypeStruct(out.shape, BF16),
        ),
        in_specs=[vmem] * 2,
        out_specs=(hbm, hbm),
        scratch_shapes=[pltpu.SemaphoreType.DMA((2,))],
        compiler_params=pltpu.CompilerParams(vmem_limit_bytes=48 * 1024 * 1024),
        cost_estimate=pl.CostEstimate(flops=0, bytes_accessed=2 * 10**6, transcendentals=0),
    )(spec, out)
    return jnp.transpose(spec, (0, 2, 1, 3)), jnp.transpose(out, (0, 1, 3, 2))


def solution(mesh):
    wave = P(None, "lev", "wave", None)
    return jax.shard_map(
        body,
        mesh=mesh,
        in_specs=(wave, wave, P("wave", None, None)) + (P(),) * 8,
        out_specs=(wave, wave),
        check_vma=False,
    )
```

```python
import functools

import jax
import jax.numpy as jnp
from jax import lax
from jax.experimental import pallas as pl
from jax.experimental.pallas import tpu as pltpu
from jax.sharding import PartitionSpec as P

MMAX = 1280
BLOCK = 64
K = 8
CHUNK = 16
F32, BF16 = jnp.float32, jnp.bfloat16
MESH = pl.DeviceIdType.MESH
HI = lax.Precision.HIGHEST
NT = (((1,), (1,)), ((), ()))


def iota(shape, dim):
    return lax.broadcasted_iota(jnp.int32, shape, dim)


def dot(a, b):
    return jnp.dot(a, b, preferred_element_type=F32)


def fdot(a, b):
    return jnp.dot(a, b, precision=HI, preferred_element_type=F32)


def onehot(mask, dtype=BF16):
    return jnp.where(mask, 1.0, 0.0).astype(dtype)


def split3(left, right):
    lh = left.astype(BF16)
    ll = (left - lh.astype(F32)).astype(BF16)
    rh = right.astype(BF16)
    rl = (right - rh.astype(F32)).astype(BF16)
    return jnp.concatenate([lh, lh, ll], axis=1), jnp.concatenate([rh, rl, rh], axis=0)


def make_slots(lev_n):
    fill = -2 * lev_n % K
    rest = list(range(fill, lev_n))
    whole = len(rest) // K * K
    slots = []
    for levels in (rest[:whole], rest[whole:]):
        for c in range(2):
            slots += [(0, l, c) for l in levels]
    groups = [slots[i : i + K] for i in range(0, len(slots), K)]
    ends = [0, len(groups)]
    for c in range(2):
        slots = [(f, l, c) for f in (1, 2) for l in range(lev_n)] + [(0, l, c) for l in range(fill)]
        groups += [slots[i : i + K] for i in range(0, len(slots), K)]
        ends.append(len(groups))
    return groups, ends


def make_pieces(lev_n, jl):
    groups, ends = make_slots(lev_n)
    count = len(groups)
    lanes = (count * jl + 127) // 128 * 128
    pad = -ends[1] * jl % 128
    if count * jl + pad > lanes:
        pad = 0
    first = [g * jl + (pad if g >= ends[1] else 0) for g in range(count)] + [lanes]
    stops = [first[ends[1]], first[ends[2]], lanes]
    up = [min((e + 127) // 128 * 128, lanes) for e in stops]
    down = [e // 128 * 128 for e in stops]
    return groups, ends, lanes, first, [0] + up, [0] + down


def lane_parts(first, jl, lo, hi):
    parts, at = [], lo
    while at < hi:
        g = max(i for i in range(len(first) - 1) if first[i] <= at)
        if at < first[g] + jl:
            stop = min(hi, first[g] + jl)
            parts.append((g, at - first[g], stop - first[g]))
        else:
            stop = min(hi, first[g + 1])
            parts.append((None, 0, stop - at))
        at = stop
    return parts


def kernel(
    n, nlev, x_hbm, old_hbm, leg_hbm, g_hbm, mi_hbm, mo_hbm, mh_hbm, rates_hbm, pid_hbm, lat_hbm, lim_hbm,
    spec_ref, out_ref,
    x_ref, old_ref, leg, g_ref, mi_ref, mo_ref, mh_ref, rates_ref, pid_ref, lat_ref, lim_ref,
    send1, recv1, send2, recv2, es, er, hot, turned,
    in_sem, s1, r1, s2, r2, es_sem, er_sem,
):
    lev_n = x_ref.shape[1]
    jl = x_ref.shape[3]
    groups, ends, lanes, base, up, down = make_pieces(lev_n, jl)
    nr, nlat = leg_hbm.shape[1:]
    me, lev = lax.axis_index("wave"), lax.axis_index("lev")
    other = lax.rem(lev + 1, nlev)

    pairs = [(x_hbm.at[f], x_ref.at[f]) for f in (0, 1, 2)] + [
        (pid_hbm, pid_ref), (lat_hbm, lat_ref), (lim_hbm, lim_ref), (g_hbm, g_ref), (mi_hbm, mi_ref),
        (mo_hbm, mo_ref), (mh_hbm, mh_ref), (rates_hbm, rates_ref), (old_hbm, old_ref), (leg_hbm.at[0], leg),
    ]
    loads = [pltpu.make_async_copy(src, dst, in_sem.at[i]) for i, (src, dst) in enumerate(pairs)]
    for load in loads[:3]:
        load.start()
    plane = n // 4

    def away(i):
        return lax.bitwise_xor(me, jnp.where((lev == 0) & (i % 2 == 0), n - 1 - i // 2, jnp.where(lev == 0, 1 + i // 2, n - 1 - i)))

    def upwards(i):
        return jnp.where(i < me, i, i + 1)

    barrier = pltpu.get_barrier_semaphore()

    def greet(i, carry):
        pl.semaphore_signal(barrier, inc=1, device_id=(upwards(i), lev), device_id_type=MESH)
        return carry

    lax.fori_loop(0, n - 1, greet, 0)
    pl.semaphore_signal(barrier, inc=1, device_id=(me, other), device_id_type=MESH)
    for load in loads[3:]:
        load.start()

    pr, pc = iota((CHUNK * 16, 1), 0), iota((1, 4 * CHUNK * K), 1)
    home = pr % K * (4 * CHUNK) + pr // 16 * 4 + pr // 8 % 2 * 2

    def perm_of(g):
        part = jnp.zeros(pr.shape, jnp.int32)
        for k, (f, l, c) in enumerate(groups[g]):
            if c:
                part = jnp.where(pr % K == k, 1, part)
        return onehot(pc == home + part)

    def parts_of(g):
        return tuple(c for f, l, c in groups[g])

    perms = {}
    for g in range(len(groups)):
        if parts_of(g) not in perms:
            perms[parts_of(g)] = perm_of(g)

    def packed(g, h):
        blocks = [x_ref[f, l, h * 4 * CHUNK : (h + 1) * 4 * CHUNK] for f, l, c in groups[g]]
        blocks += [jnp.zeros_like(blocks[0])] * (K - len(blocks))
        return jnp.concatenate(blocks, axis=0)

    def pack_run(first, last, h):
        out, g = [], first
        while g < last:
            run = [g]
            while run[-1] + 1 < last and parts_of(run[-1] + 1) == parts_of(g):
                run.append(run[-1] + 1)
            data = [packed(i, h) for i in run]
            data = jnp.concatenate(data, axis=1) if len(run) > 1 else data[0]
            data = dot(perms[parts_of(g)], data).astype(BF16)
            out += [data[:, i * jl : (i + 1) * jl] for i in range(len(run))]
            g = run[-1] + 1
        return out

    def copy1(p, to):
        at = pl.ds(up[p], up[p + 1] - up[p])
        return pltpu.make_async_remote_copy(
            src_ref=send1.at[to, :, at], dst_ref=recv1.at[me, :, at], send_sem=s1.at[0], recv_sem=r1.at[p],
            device_id=(to, lev), device_id_type=MESH,
        )

    def copy2(p, to):
        at = pl.ds(down[p], down[p + 1] - down[p])
        return pltpu.make_async_remote_copy(
            src_ref=send2.at[to, :, at], dst_ref=recv2.at[me, :, at], send_sem=s2.at[0], recv_sem=r2.at[p + me // plane if p == 2 else p],
            device_id=(to, lev), device_id_type=MESH,
        )

    def start_all(copy, p, order):
        def start(i, carry):
            copy(p, order(i)).start()
            return carry

        lax.fori_loop(0, n - 1, start, 0)

    def whole(src, dst, bounds, ss, rr, p):
        at = pl.ds(bounds[p], bounds[p + 1] - bounds[p])
        return pltpu.make_async_remote_copy(
            src_ref=src.at[pl.ds(0, n - 1), :, at], dst_ref=dst.at[pl.ds(0, n - 1), :, at], send_sem=ss.at[0],
            recv_sem=rr.at[p], device_id=(me, other), device_id_type=MESH,
        )

    done = 0
    held = {}
    for p in range(3):
        lo, hi = up[p], up[p + 1]
        if p == 0:
            loads[0].wait()
        if p == 1:
            loads[1].wait()
            loads[2].wait()
        if hi == lo:
            continue
        parts = lane_parts(base, jl, lo, hi)
        last = max([g + 1 for g, u, v in parts if g is not None] + [done])
        for h in range(n // CHUNK):
            held.update({(h, done + i): x for i, x in enumerate(pack_run(done, last, h))})
            row = [
                jnp.zeros((CHUNK * 16, v), BF16) if g is None else held[h, g][:, u:v] for g, u, v in parts
            ]
            row = jnp.concatenate(row, axis=1) if len(row) > 1 else row[0]
            send1[h * CHUNK : (h + 1) * CHUNK, :, lo:hi] = row.reshape(CHUNK, 16, hi - lo)
        done = last
        if p == 0:
            pl.semaphore_wait(barrier, n)
        start_all(copy1, p, away)
        recv1[me, :, lo:hi] = send1[me, :, lo:hi]

    for load in loads[3:12]:
        load.wait()

    hr = iota((16, nlat), 0)
    lim = lim_ref[...][None, :]
    lim_rows = jnp.where(hr == 0, lim // 8, jnp.where(hr == 1, lim % 8, 0)).astype(F32).astype(BF16)
    hot[...] = onehot(iota((nlat, nlat), 0) == lat_ref[...][None, :])
    got = dot(lim_rows, hot[...])
    row_limit = got[0:1] * 8.0 + got[1:2]
    a = pid_ref[me]
    wave = jnp.where(hr < 8, a, MMAX - 1 - a).astype(F32)
    keep = onehot(wave < row_limit, F32)
    keep_b = keep.astype(BF16)

    r = iota((1, nr), 1)
    first_pad = (MMAX - a + BLOCK - 1) // BLOCK * BLOCK
    first = r < first_pad
    used = (first & (r < MMAX - a)) | ((r >= first_pad) & (r - first_pad <= a))
    degree = jnp.where(first, a + r, MMAX - 1 - a + r - first_pad).astype(F32)
    lam = degree * (degree + 1.0) / float(MMAX * (MMAX - 1))

    levels = nlev * lev_n
    half = (levels + 15) // 16 * 16
    td = (ends[2] - ends[1]) * K
    mode = onehot(iota((half, levels), 0) == iota((half, levels), 1), F32)
    mode_t = onehot(iota((levels, half), 0) == iota((levels, half), 1), F32)
    own = lev_n * lev
    li, si = iota((levels, td), 0), iota((levels, td), 1)
    pick_div = onehot((li == own + si) & (si < lev_n), F32)
    pick_heat = onehot((li == own + si - lev_n) & (si >= lev_n) & (si < 2 * lev_n), F32)
    si, li = iota((td, levels), 0), iota((td, levels), 1)
    pick_div_t = onehot((li == own + si) & (si < lev_n), F32)
    pick_heat_t = onehot((li == own + si - lev_n) & (si >= lev_n) & (si < 2 * lev_n), F32)
    m_in = mi_ref[...]
    w1 = jnp.concatenate(
        [fdot(fdot(mode, m_in), pick_div), fdot(fdot(mode, fdot(m_in, g_ref[...])), pick_heat)], axis=0
    )
    w2 = fdot(fdot(pick_div_t, mo_ref[...]), mode_t) - 2.0 * fdot(fdot(pick_heat_t, mh_ref[...]), mode_t)
    rates = jnp.sum(
        jnp.where(iota((half, levels), 0) == iota((half, levels), 1), rates_ref[...][None, :], 0.0),
        axis=1, keepdims=True,
    )
    si = iota((td, 1), 0)
    stays = onehot(si >= lev_n, F32)

    def old_rows(p):
        slots = [s for g in groups[ends[p] : ends[p + 1]] for s in g]
        rows = (ends[p + 1] - ends[p]) * K
        total = None
        for c in range(2):
            if not any(s[2] == c for s in slots):
                continue
            row, col = iota((rows, 3 * lev_n), 0), iota((rows, 3 * lev_n), 1)
            src = jnp.full(row.shape, -1, jnp.int32)
            start = 0
            while start < len(slots):
                f, l, cc = slots[start]
                stop = start
                while stop < len(slots) and slots[stop] == (f, l + stop - start, cc):
                    stop += 1
                if cc == c:
                    src = jnp.where((row >= start) & (row < stop), row - start + f * lev_n + l, src)
                start = stop
            part = dot(onehot(col == src), old_all[:, c * nr : (c + 1) * nr])
            total = part if total is None else total + part
        return total

    old_all = jnp.concatenate([old_ref[f, 0] for f in range(3)], axis=0)
    olds = [old_rows(p) for p in range(3)]
    loads[12].wait()

    def turn(i, carry):
        at = pl.ds(pl.multiple_of(i * 128, 128), 128)
        turned[:, at] = leg[at, :].T
        return carry

    lax.fori_loop(0, nr // 128, turn, 0)

    def forward(p):
        g_n = ends[p + 1] - ends[p]
        cols = jnp.concatenate(
            [
                jnp.concatenate([recv1[d, :, base[g] : base[g] + jl] for d in range(n)], axis=1) * keep_b
                for g in range(ends[p], ends[p + 1])
            ],
            axis=0,
        )
        both = dot(cols, turned[...]).reshape(g_n, 2, K, nr)
        total = jnp.where(iota((g_n, K, nr), 2) < first_pad, both[:, 0], both[:, 1]).reshape(g_n * K, nr)
        return jnp.where(used, olds[p] + total, 0.0)

    def inverse(p, new):
        g_n = ends[p + 1] - ends[p]
        sides = jnp.stack(
            [
                jnp.where(first, new, 0.0).reshape(g_n, K, nr),
                jnp.where(first, 0.0, new).reshape(g_n, K, nr),
            ],
            axis=1,
        ).reshape(g_n * 16, nr).astype(BF16)
        out = dot(sides, leg[...])
        return [(out[i * 16 : (i + 1) * 16] * keep).astype(BF16) for i in range(g_n)]

    def exchange(p):
        return pltpu.make_async_remote_copy(
            src_ref=es.at[p], dst_ref=er.at[p], send_sem=es_sem.at[p], recv_sem=er_sem.at[p],
            device_id=(me, other), device_id_type=MESH,
        )

    grids = []

    def fill_piece(p):
        lo, hi = down[p], down[p + 1]
        for d in range(n if hi > lo else 0):
            row = [
                jnp.zeros((16, v), BF16) if g is None else grids[g][:, d * jl + u : d * jl + v]
                for g, u, v in lane_parts(base, jl, lo, hi)
            ]
            send2[d, :, lo:hi] = jnp.concatenate(row, axis=1) if len(row) > 1 else row[0]

    def send_piece(p):
        if down[p + 1] > down[p]:
            start_all(copy2, p, upwards if p else away)

    def arrive(p):
        if up[p + 1] > up[p]:
            whole(send1, recv1, up, s1, r1, p).wait_recv()

    def project(p, total):
        w1s, ts = split3(w1, total)
        res = dot(w1s, ts)
        proj = res[:half] + 2.0 * lam * res[half:]
        es[p - 1] = proj.astype(BF16)
        exchange(p - 1).start()
        return proj

    def step(p, total, proj):
        exchange(p - 1).wait()
        modal = (proj + er[p - 1].astype(F32)) / (1.0 + 4.0 * lam * rates)
        w2s, ms = split3(w2, modal)
        return jnp.where(used, total * stays + dot(w2s, ms), 0.0)

    arrive(0)
    vort = forward(0)
    grids += inverse(0, vort)
    fill_piece(0)
    arrive(1)
    total1 = forward(1)
    proj1 = project(1, total1)
    send_piece(0)
    arrive(2)
    total2 = forward(2)
    proj2 = project(2, total2)
    new1 = step(1, total1, proj1)
    grids += inverse(1, new1)
    fill_piece(1)
    send_piece(1)
    new2 = step(2, total2, proj2)
    grids += inverse(2, new2)
    fill_piece(2)
    send_piece(2)
    news = [vort, new1, new2]

    flat = [s for g in groups for s in g + [None] * (K - len(g))]
    starts = [e * K for e in ends]

    def row_of(slot):
        i = flat.index(slot)
        p = max(j for j in range(3) if starts[j] <= i)
        return p, i - starts[p]

    for c in range(2):
        for f in range(3):
            parts, l = [], 0
            while l < lev_n:
                p, i = row_of((f, l, c))
                stop = l
                while stop < lev_n and row_of((f, stop, c)) == (p, i + stop - l):
                    stop += 1
                parts.append(news[p][i : i + stop - l])
                l = stop
            rows = jnp.concatenate(parts, axis=0) if len(parts) > 1 else parts[0]
            spec_ref[f, 0, :, c * nr : (c + 1) * nr] = rows.astype(BF16)
    qr, qc = iota((4 * CHUNK * K, 1), 0), iota((1, CHUNK * 16), 1)
    q = qr % (4 * CHUNK)
    home = q // 4 * 16 + q // 2 % 2 * 8 + qr // (4 * CHUNK)
    backs = [onehot(qc == jnp.where(q % 2 == c, home, -1)) for c in range(2)]
    where = {s: (g, k) for g, slots in enumerate(groups) for k, s in enumerate(slots)}
    paired, single = [], []
    for g, slots in enumerate(groups):
        if all(c == 0 for f, l, c in slots):
            b = where[slots[0][0], slots[0][1], 1][0]
            if all(where[f, l, 1] == (b, k) for k, (f, l, c) in enumerate(slots)):
                paired.append((g, b))
    covered = {g for pair in paired for g in pair}
    for g, slots in enumerate(groups):
        if g not in covered:
            zero = [(f, l) for f, l, c in slots if c == 0]
            count = len(zero)
            sr = iota((4 * CHUNK * count, 1), 0)
            sq = sr % (4 * CHUNK)
            single.append(
                (g, zero, onehot(qc == sq // 4 * 16 + sq // 2 % 2 * 8 + sr // (4 * CHUNK) + count * (sq % 2)))
            )

    def stage(g):
        return min(p for p in range(3) if base[g] + jl <= down[p + 1])

    def wide(p, h, run):
        rows = recv2[h * CHUNK : (h + 1) * CHUNK, :, : down[p + 1]].reshape(CHUNK * 16, down[p + 1])
        rows = [rows[:, base[g] : base[g] + jl] for g in run]
        return jnp.concatenate(rows, axis=1) if len(rows) > 1 else rows[0]

    for p in range(2):
        lo, hi = down[p], down[p + 1]
        if hi > lo:
            recv2[me, :, lo:hi] = send2[me, :, lo:hi]
            whole(send2, recv2, down, s2, r2, p).wait_recv()
        now = [(g, b) for g, b in paired if max(stage(g), stage(b)) == p]
        for h in range(n // CHUNK):
            qs = slice(h * 4 * CHUNK, (h + 1) * 4 * CHUNK)
            if now:
                got = dot(backs[0], wide(p, h, [g for g, b in now])) + dot(backs[1], wide(p, h, [b for g, b in now]))
                for i, (g, b) in enumerate(now):
                    piece = got[:, i * jl : (i + 1) * jl].astype(BF16)
                    for k, (f, l, c) in enumerate(groups[g]):
                        out_ref[f, l, qs] = piece[k * 4 * CHUNK : (k + 1) * 4 * CHUNK]
            for g, zero, perm in single:
                if stage(g) == p:
                    piece = dot(perm, wide(p, h, [g])).astype(BF16)
                    for k, (f, l) in enumerate(zero):
                        out_ref[f, l, qs] = piece[k * 4 * CHUNK : (k + 1) * 4 * CHUNK]

    whole(send1, recv1, [0, lanes], s1, r1, 0).wait_send()
    whole(send2, recv2, [0, lanes], s2, r2, 0).wait_send()

    lo, hi = down[2], down[3]
    recv2[me, :, lo:hi] = send2[me, :, lo:hi]
    now = [(g, b) for g, b in paired if max(stage(g), stage(b)) == 2]
    wide_q = 4 * plane
    qr, qc = iota((wide_q * K, 1), 0), iota((1, 2 * plane * 16), 1)
    q = qr % wide_q
    turn_back = onehot(qc == q % 2 * (plane * 16) + q // 4 * 16 + q // 2 % 2 * 8 + qr // wide_q)
    for i in range(4):
        t = lax.bitwise_xor(me // plane, i)
        count = plane if i else plane - 1
        landed = recv2.at[pl.ds(0, count), :, pl.ds(lo, hi - lo)]
        pltpu.make_async_remote_copy(
            src_ref=send2.at[pl.ds(0, count), :, pl.ds(lo, hi - lo)], dst_ref=landed, send_sem=s2.at[0],
            recv_sem=r2.at[2 + t], device_id=(me, other), device_id_type=MESH,
        ).wait_recv()
        rows = recv2[pl.ds(t * plane, plane)].reshape(plane * 16, lanes)
        data = [
            jnp.concatenate([rows[:, base[g] : base[g] + jl] for g in run], axis=1) for run in zip(*now)
        ]
        got = dot(turn_back, jnp.concatenate(data, axis=0)).astype(BF16)
        at = pl.ds(pl.multiple_of(t * wide_q, wide_q), wide_q)
        for m, (g, b) in enumerate(now):
            for k, (f, l, c) in enumerate(groups[g]):
                out_ref[f, l, at] = got[k * wide_q : (k + 1) * wide_q, m * jl : (m + 1) * jl]


def finish(spec, out, spec_hbm, out_hbm, sem):
    copies = [
        pltpu.make_async_copy(out, out_hbm, sem.at[0]),
        pltpu.make_async_copy(spec, spec_hbm, sem.at[1]),
    ]
    for copy in copies:
        copy.start()
    for copy in copies:
        copy.wait()


def body(
    fourier_in, spectral_old, legendre, g_matrix, modes_in, modes_out, mode_heating, mode_rates, pair_ids, lat_ids,
    limits,
):
    n, nlev = lax.axis_size("wave"), lax.axis_size("lev")
    fields, lev_n, jl, q_n = fourier_in.shape
    groups, ends, lanes, base, up, down = make_pieces(lev_n, jl)
    nr, nlat = legendre.shape[1:]
    half = (nlev * lev_n + 15) // 16 * 16
    hbm = pl.BlockSpec(memory_space=pltpu.HBM)
    vmem = pl.BlockSpec(memory_space=pltpu.VMEM)
    spec, out = pl.pallas_call(
        functools.partial(kernel, n, nlev),
        out_shape=(
            jax.ShapeDtypeStruct((fields, 1, lev_n, 2 * nr), BF16),
            jax.ShapeDtypeStruct((fields, lev_n, q_n, jl), BF16),
        ),
        in_specs=[hbm] * 11,
        out_specs=(vmem, vmem),
        scratch_shapes=[
            pltpu.VMEM((fields, lev_n, q_n, jl), BF16),
            pltpu.VMEM((fields, 1, lev_n, 2 * nr), BF16),
            pltpu.VMEM((nr, nlat), BF16),
            pltpu.VMEM(g_matrix.shape, F32),
            pltpu.VMEM(g_matrix.shape, F32),
            pltpu.VMEM(g_matrix.shape, F32),
            pltpu.VMEM(g_matrix.shape, F32),
            pltpu.VMEM(mode_rates.shape, F32),
            pltpu.SMEM(pair_ids.shape, jnp.int32),
            pltpu.VMEM(lat_ids.shape, jnp.int32),
            pltpu.VMEM(limits.shape, jnp.int32),
            pltpu.VMEM((n, 16, lanes), BF16),
            pltpu.VMEM((n, 16, lanes), BF16),
            pltpu.VMEM((n, 16, lanes), BF16),
            pltpu.VMEM((n, 16, lanes), BF16),
            pltpu.VMEM((2, half, nr), BF16),
            pltpu.VMEM((2, half, nr), BF16),
            pltpu.VMEM((nlat, nlat), BF16),
            pltpu.VMEM((nlat, nr), BF16),
            pltpu.SemaphoreType.DMA((13,)),
            pltpu.SemaphoreType.DMA((1,)),
            pltpu.SemaphoreType.DMA((3,)),
            pltpu.SemaphoreType.DMA((1,)),
            pltpu.SemaphoreType.DMA((6,)),
            pltpu.SemaphoreType.DMA((2,)),
            pltpu.SemaphoreType.DMA((2,)),
        ],
        compiler_params=pltpu.CompilerParams(
            collective_id=0, has_side_effects=True, vmem_limit_bytes=48 * 1024 * 1024
        ),
        cost_estimate=pl.CostEstimate(flops=10**9, bytes_accessed=8 * 10**6, transcendentals=0),
    )(
        *[
            pltpu.with_memory_space_constraint(x, pltpu.HBM)
            for x in (
                jnp.transpose(fourier_in, (0, 1, 3, 2)),
                jnp.transpose(spectral_old, (0, 2, 1, 3)),
                legendre,
                g_matrix,
                modes_in,
                modes_out,
                mode_heating,
                mode_rates,
                pair_ids,
                lat_ids,
                limits,
            )
        ]
    )
    spec, out = pl.pallas_call(
        finish,
        out_shape=(
            jax.ShapeDtypeStruct(spec.shape, BF16),
            jax.ShapeDtypeStruct(out.shape, BF16),
        ),
        in_specs=[vmem] * 2,
        out_specs=(hbm, hbm),
        scratch_shapes=[pltpu.SemaphoreType.DMA((2,))],
        compiler_params=pltpu.CompilerParams(vmem_limit_bytes=48 * 1024 * 1024),
        cost_estimate=pl.CostEstimate(flops=0, bytes_accessed=2 * 10**6, transcendentals=0),
    )(spec, out)
    return jnp.transpose(spec, (0, 2, 1, 3)), jnp.transpose(out, (0, 1, 3, 2))


def solution(mesh):
    wave = P(None, "lev", "wave", None)
    return jax.shard_map(
        body,
        mesh=mesh,
        in_specs=(wave, wave, P("wave", None, None)) + (P(),) * 8,
        out_specs=(wave, wave),
        check_vma=False,
    )
```
